128 devices in a mesh: blk: 16 (over z, y), rows: 8 (over x, core).
Axes of the slice: x: 4, y: 4, z: 4, core: 2. Of those that a mesh axis runs over, the one named last changes fastest.
Arguments:
- fine_blocks: bfloat16 [8, 16, 16, 8, 128, 128], P('rows', 'blk'), may hold values from -0.5 to 0.5
- block_rows: int32 [8, 16, 16, 8], P('rows', 'blk'), may hold values from 0 to 15
- block_cols: int32 [8, 16, 16, 8], P('rows', 'blk'), may hold values from 0 to 15
- block_counts: int32 [8, 16, 16], P('rows', 'blk'), may hold values from 1 to 8, 72 in all within a row
- prolong_blocks: bfloat16 [8, 256, 128, 384], P('rows', 'blk'), may hold values from -1.1953125 to 1.1953125
- prolong_mask: int32 [8, 256, 3], P('rows', 'blk'), may hold values 0 or 1
Outputs:
- coarse_blocks: float32 [8, 16, 128, 16, 5, 128], P('rows', 'blk')
The draws below stay inside these ranges and needn't reach their ends.
Inputs may be any that keep to these rules, and one draw needn't show every extreme that they name: `block_counts`: the 16 counts of one device sum to 72, and one of them is 8.
All inputs are finite; a program needn't handle non-finite values. No bound on the sum of `prolong_mask` on one device may be relied on, other than what follows from the above.
Results may differ from the reference program's by a relative error of at most 0.004.
Values may be sent and summed in bfloat16 or wider, within the bound.
A program may use at most 128 MiB of HBM per device.

```python
import math
import jax
import jax.numpy as jnp
import numpy as np
from jax import lax

PORES = 128
CDOF = 128
ROWS_DEV = 16
CAP = 8
LIVE = 72
GROUP_ROWS = 256
N_BLK = 16
N_ROWS = 8


def touch_ends(values, own_key, smallest, largest):
    shape = values.shape
    place = [jax.random.randint(jax.random.fold_in(own_key, axis), (), 0, shape[axis]) for axis in range(len(shape))]
    values = values.at[tuple(place)].set(smallest)
    longest = shape.index(max(shape))
    place[longest] = (place[longest] + 1) % shape[longest]
    return values.at[tuple(place)].set(largest)


def shard_levels(stream_key, shape, pieces, smallest, largest):
    def one(axis_at, parts):
        heights = jax.random.uniform(jax.random.fold_in(jax.random.fold_in(stream_key, 6), axis_at), (parts,), jnp.float32, smallest / len(pieces), largest / len(pieces))
        return jnp.repeat(jnp.exp(heights), shape[axis_at] // parts).reshape((-1,) + (1,) * (len(shape) - axis_at - 1))

    gain = one(*pieces[0])
    for cut in pieces[1:]:
        gain = gain * one(*cut)
    return gain


def split_up(amount, total, bound, slope):
    loads = [(1 << 20) // math.isqrt(grade ** slope) + 1 for grade in range(2, amount + 1)]
    spare, counts = total - bound - (amount - 1), [1] * (amount - 1)
    while spare > 0:
        free = [i for i in range(amount - 1) if counts[i] < bound]
        whole, remaining = sum([loads[i] for i in free]), spare
        for i in free:
            extra = min(bound - counts[i], max(1, remaining * loads[i] // whole), spare)
            counts[i] = counts[i] + extra
            spare = spare - extra
    return np.array([bound] + counts)


def uneven(rng, number_of, total, bound, skew):
    if number_of == 2:
        one = jax.random.randint(rng, (), max(1, total - bound), min(bound, total - 1) + 1)
        return jnp.stack([one, total - one])
    sizes = jnp.asarray(split_up(number_of, total, bound, skew), jnp.int32)
    twos = (number_of - 1) // 2
    giver, receiver = sizes[1:1 + 2 * twos:2], sizes[2:2 + 2 * twos:2]
    margin = jnp.minimum(giver - 1, bound - receiver)
    shifted = jax.random.randint(jax.random.fold_in(rng, 1), (twos,), 0, 1 << 20) % (margin + 1)
    sizes = sizes.at[1:1 + 2 * twos:2].set(giver - shifted).at[2:2 + 2 * twos:2].set(receiver + shifted)
    return sizes[jax.random.permutation(jax.random.fold_in(rng, 2), number_of)]


def normal_values(own_key, extent, deviation, limit, split=(), held_as=jnp.bfloat16):
    gain = shard_levels(own_key, extent, split, -0.22, 0.18) if split else 1.0
    result = jax.random.normal(own_key, extent, jnp.float32) * deviation * gain
    return jnp.minimum(jnp.maximum(result, -limit), limit).astype(held_as)


def setup_inputs(seed: int = 0) -> dict:
    streams_of = jax.random.split(jax.random.key(seed), 7)
    fine_blocks = normal_values(streams_of[0], (N_ROWS, N_BLK, N_BLK, CAP, PORES, PORES), PORES ** -0.5, 0.5, ((0, 8), (1, 16)))
    block_rows = touch_ends(jax.random.randint(streams_of[1], (N_ROWS, N_BLK, N_BLK, CAP), 0, ROWS_DEV), jax.random.fold_in(streams_of[1], 1), 0, ROWS_DEV - 1).astype(jnp.int32)
    block_cols = touch_ends(jax.random.randint(streams_of[2], (N_ROWS, N_BLK, N_BLK, CAP), 0, ROWS_DEV), jax.random.fold_in(streams_of[2], 1), 0, ROWS_DEV - 1).astype(jnp.int32)
    block_counts = jax.vmap(lambda own: uneven(own, N_BLK, LIVE, CAP, 2))(jax.random.split(streams_of[3], N_ROWS * N_BLK)).reshape((N_ROWS, N_BLK, N_BLK)).astype(jnp.int32)
    prolong_blocks = normal_values(streams_of[4], (N_ROWS, GROUP_ROWS, PORES, 3 * CDOF), 0.2, 1.1953125, ((0, 8), (1, 16)))
    prolong_mask = touch_ends((jax.random.randint(streams_of[5], (N_ROWS, GROUP_ROWS, 3), 0, 3) < 2).astype(jnp.int32), jax.random.fold_in(streams_of[5], 1), 0, 1)
    return dict(fine_blocks=fine_blocks, block_rows=block_rows, block_cols=block_cols, block_counts=block_counts, prolong_blocks=prolong_blocks, prolong_mask=prolong_mask)


def masked_prolong(prolong_blocks, prolong_mask):
    groups = jnp.arange(N_ROWS, dtype=jnp.int32)[:, None, None]
    target = groups + jnp.arange(3, dtype=jnp.int32)[None, None, :] - 1
    keeper = (prolong_mask == 1) & (target >= 0) & (target < N_ROWS)
    reshaped_blocks = prolong_blocks.reshape(N_ROWS, GROUP_ROWS, PORES, 3, CDOF)
    kept_blocks = reshaped_blocks * keeper[:, :, None, :, None].astype(prolong_blocks.dtype)
    return kept_blocks.reshape(N_ROWS, GROUP_ROWS, PORES, 3 * CDOF)


def reference(fine_blocks, block_rows, block_cols, block_counts, prolong_blocks, prolong_mask):
    valid_rows = masked_prolong(prolong_blocks, prolong_mask)

    def one_device(device_index):
        group_index = (device_index // N_BLK).astype(jnp.int32)
        panel_index = (device_index % N_BLK).astype(jnp.int32)
        group_rows = lax.dynamic_index_in_dim(valid_rows, group_index, 0, keepdims=False)
        slot_blocks = lax.dynamic_index_in_dim(lax.dynamic_index_in_dim(fine_blocks, group_index, 0, keepdims=False), panel_index, 0, keepdims=False)
        slot_rows = lax.dynamic_index_in_dim(lax.dynamic_index_in_dim(block_rows, group_index, 0, keepdims=False), panel_index, 0, keepdims=False)
        slot_cols = lax.dynamic_index_in_dim(lax.dynamic_index_in_dim(block_cols, group_index, 0, keepdims=False), panel_index, 0, keepdims=False)
        slot_counts = lax.dynamic_index_in_dim(lax.dynamic_index_in_dim(block_counts, group_index, 0, keepdims=False), panel_index, 0, keepdims=False)
        global_rows = (jnp.arange(N_BLK, dtype=jnp.int32)[:, None] * ROWS_DEV + slot_cols).astype(jnp.int32)
        chosen_entries = jnp.take(group_rows, global_rows, axis=0)
        block_products = jnp.einsum("ptab,ptbc->ptac", slot_blocks.astype(jnp.float32), chosen_entries.astype(jnp.float32))
        is_live = jnp.arange(CAP, dtype=jnp.int32)[None, :] < slot_counts[:, None]
        selector_mask = ((slot_rows[:, :, None] == jnp.arange(ROWS_DEV, dtype=jnp.int32)[None, None, :]) & is_live[:, :, None]).astype(jnp.float32)
        operator_prolong_blocks = jnp.einsum("pti,ptac->iapc", selector_mask, block_products, precision=lax.Precision.HIGHEST).astype(jnp.bfloat16)
        own_rows = lax.dynamic_slice_in_dim(group_rows, (panel_index * ROWS_DEV).astype(jnp.int32), ROWS_DEV, 0)
        partial_value = jnp.dot(own_rows.reshape(ROWS_DEV * PORES, 3 * CDOF).T, operator_prolong_blocks.reshape(ROWS_DEV * PORES, N_BLK * 3 * CDOF), preferred_element_type=jnp.float32)
        return partial_value.astype(jnp.bfloat16).reshape(3, CDOF, N_BLK, 3, CDOF)

    partial_all = lax.map(one_device, jnp.arange(N_ROWS * N_BLK, dtype=jnp.int32))
    partial_all = partial_all.reshape(N_ROWS, N_BLK, 3, CDOF, N_BLK, 3, CDOF)
    own_part = partial_all[:, :, 1].astype(jnp.float32)
    empty_rim = jnp.zeros((1, N_BLK, CDOF, N_BLK, 3, CDOF), jnp.float32)
    from_lower = jnp.concatenate([empty_rim, partial_all[:-1, :, 2].astype(jnp.float32)], axis=0)
    from_upper = jnp.concatenate([partial_all[1:, :, 0].astype(jnp.float32), empty_rim], axis=0)
    widths_own = ((0, 0), (0, 0), (0, 0), (0, 0), (1, 1), (0, 0))
    widths_low = ((0, 0), (0, 0), (0, 0), (0, 0), (0, 2), (0, 0))
    widths_up = ((0, 0), (0, 0), (0, 0), (0, 0), (2, 0), (0, 0))
    return jnp.pad(own_part, widths_own) + jnp.pad(from_lower, widths_low) + jnp.pad(from_upper, widths_up)
```

```python
import jax
import jax.numpy as jnp
from jax import lax
from jax.experimental import pallas as pl
from jax.experimental.pallas import tpu as pltpu
from jax.sharding import PartitionSpec as P

MESH = pl.DeviceIdType.MESH
BF16 = jnp.bfloat16
F32 = jnp.float32
SIDE = 4
ROWS = 16
CAP = 8
PORES = 128
HALF = 64
WIDTH = 384
GROUPS = 8
PANELS = 16
T_ROWS, T_COUNT, T_MASK, T_ALL = 8, 16, 17, 24


def panel_order(i):
    late = i // 9
    a, b = i // 3, i % 3
    near_z, near_y = a + a // 2, b + b // 2
    k = i + 9 - 18 * late
    s = k // 2
    s = s + s // 2 - 2 * (i // 15)
    odd = k % 2
    far_z = (1 - odd) * s + 2 * odd
    far_y = (1 - odd) * 2 + odd * s
    return near_z * (1 - late) + far_z * late, near_y * (1 - late) + far_y * late


def kernel(
    fine, table, prolong, out,
    stage, amat, vt, yg0, yg1, yg2, yg3, zg0, zg1, zg2, zg3,
    right, pack, relay, tabs, tabs_s, near_s, own, give, got, lt, mid,
    load_sem, tab_send, tab_recv, tab_sem, ring_send, ring_recv, pack_send, relay_send, relay_recv, right_recv,
    give_send, got_recv,
):
    blk, g = lax.axis_index("blk"), lax.axis_index("rows")
    z, y = blk // SIDE, blk % SIDE

    def at(dz, dy):
        return ((z + dz) % SIDE) * SIDE + (y + dy) % SIDE

    def along(axis, d):
        return (at(0, d), g) if axis == 0 else (at(d, 0), g)

    below, above = (blk, (g + GROUPS - 1) % GROUPS), (blk, (g + 1) % GROUPS)

    load_v = pltpu.make_async_copy(prolong, stage, load_sem.at[0])
    load_v.start()
    load_a = pltpu.make_async_copy(fine, amat, load_sem.at[1])
    load_a.start()
    load_t = pltpu.make_async_copy(table, tabs_s, load_sem.at[2])
    load_t.start()

    barrier = pltpu.get_barrier_semaphore()
    friends = [along(axis, d) for axis in range(2) for d in (1, 2, 3)] + [below, above]
    for friend in friends:
        pl.semaphore_signal(barrier, inc=1, device_id=friend, device_id_type=MESH)
    pl.semaphore_wait(barrier, len(friends))

    def remote(src, dst, send, recv, device):
        return pltpu.make_async_remote_copy(
            src_ref=src, dst_ref=dst, send_sem=send, recv_sem=recv, device_id=device, device_id_type=MESH
        )

    sent = []

    def send(*args):
        copy = remote(*args)
        copy.start()
        sent.append(copy)
        return copy

    for axis in range(2):
        for d in (1, 2, 3):
            there = axis * 3 + (SIDE - d) - 1
            here = axis * 3 + d - 1
            copy = remote(
                table.at[pl.ds(0, 8)], tabs.at[there], tab_send.at[here], tab_recv.at[there], along(axis, d)
            )
            copy.start()
            sent.append(copy)

    load_t.wait()
    load_v.wait()

    def mask_row(j, carry):
        blocks = []
        for e in range(3):
            inside = jnp.logical_and(g + e - 1 >= 0, g + e - 1 < GROUPS)
            keep = jnp.logical_and(tabs_s[T_MASK + e, j] == 1, inside)
            keep = jnp.full((PORES, PORES), jnp.where(keep, 1.0, 0.0), F32).astype(BF16)
            blocks.append(stage[j, :, pl.ds(e * PORES, PORES)] * keep)
        row = jnp.concatenate(blocks, axis=1)
        yg0[j] = row[:HALF]
        zg0[j] = row[HALF:]
        return carry

    lax.fori_loop(0, ROWS, mask_row, 0)

    rings = ((yg0, yg1, yg2, yg3), (zg0, zg1, zg2, zg3))
    low, high = pl.ds(0, 8), pl.ds(8, 8)

    def ring_copy(axis, kind):
        r = rings[axis]
        up, down = along(axis, 1), along(axis, 3)
        src, dst, device = {
            0: (r[0].at[low], r[3].at[low], up),
            1: (r[0].at[high], r[1].at[high], down),
            2: (r[0].at[high], r[3].at[high], up),
            3: (r[0].at[low], r[1].at[low], down),
            4: (r[3].at[low], r[2].at[low], up),
            5: (r[1].at[high], r[2].at[high], down),
        }[kind]
        return remote(src, dst, ring_send.at[axis, kind], ring_recv.at[axis, kind], device)

    ring = {(axis, kind): ring_copy(axis, kind) for axis in range(2) for kind in range(6)}
    for kind in range(4):
        for axis in range(2):
            ring[axis, kind].start()

    def turn(j, carry):
        row = jnp.concatenate([yg0[j], zg0[j]], axis=0)
        vt[j] = row.T
        return carry

    lax.fori_loop(0, ROWS, turn, 0)

    for axis in range(2):
        for d in (1, 2, 3):
            slot = axis * 3 + d - 1
            remote(
                table.at[pl.ds(0, 8)], tabs.at[slot], tab_send.at[slot], tab_recv.at[slot], along(axis, d)
            ).wait_recv()
    load_c = pltpu.make_async_copy(tabs, near_s, tab_sem)
    load_c.start()
    load_c.wait()

    def fill(dst, axis, d, who, panel):
        src = rings[axis][d]

        def one(t, carry):
            column = tabs_s[t, panel] if who is None else near_s[who, t, panel]
            dst[t] = src[column]
            return carry

        lax.fori_loop(0, CAP, one, 0)

    def place(axis, d, far):
        return (axis, far, d) if axis == 0 else (axis, d, far)

    def panel_of(axis, d):
        return at(0, d) if axis == 0 else at(d, 0)

    def post(axis, d, t):
        other = 1 - axis
        who = other * 3 + t - 1
        slot = pack.at[axis, t - 1, d]
        fill(slot, axis, d, who, panel_of(axis, d))
        send_sem = pack_send.at[axis, t - 1, d]
        if t == 2:
            way = 0 if d in (0, 1) else 1
            n = 0 if d in (0, 3) else 1
            send(slot, relay.at[axis, way, n], send_sem, relay_recv.at[axis, way, n], along(other, 1 if way == 0 else 3))
        else:
            where = place(axis, d, SIDE - t)
            send(slot, right.at[where], send_sem, right_recv.at[where], along(other, t))

    def keep(axis, d):
        fill(right.at[place(axis, d, 0)], axis, d, None, panel_of(axis, d))

    def post_all(d):
        for t in (2, 1, 3):
            for axis in range(2):
                post(axis, d, t)

    for axis in range(2):
        keep(axis, 0)
    for axis in range(2):
        post(axis, 0, 2)
    for axis in range(2):
        post(axis, 0, 1)
        post(axis, 0, 3)
    for kind in (0, 1):
        for axis in range(2):
            ring[axis, kind].wait_recv()
            ring[axis, kind + 4].start()
    for kind in (2, 3):
        for axis in range(2):
            ring[axis, kind].wait_recv()
    post_all(1)
    post_all(3)

    def forward(axis, way, n):
        other = 1 - axis
        d = ((0, 1), (3, 2))[way][n]
        where = place(axis, d, 2)
        remote(
            pack.at[axis, 1, d], relay.at[axis, way, n], pack_send.at[axis, 1, d], relay_recv.at[axis, way, n],
            along(other, 1 if way == 0 else 3),
        ).wait_recv()
        send(
            relay.at[axis, way, n], right.at[where], relay_send.at[axis, way, n], right_recv.at[where],
            along(other, 1 if way == 0 else 3),
        )

    for kind in (4, 5):
        for axis in range(2):
            ring[axis, kind].wait_recv()
    post_all(2)
    for n in range(2):
        for axis in range(2):
            for way in range(2):
                forward(axis, way, n)
    for axis in range(2):
        for d in (1, 2, 3):
            keep(axis, d)

    load_a.wait()

    def gives(slot):
        return (
            remote(give.at[0, slot], got.at[0, slot], give_send.at[0, slot], got_recv.at[0, slot], below),
            remote(give.at[1, slot], got.at[1, slot], give_send.at[1, slot], got_recv.at[1, slot], above),
        )

    def product(i):
        dz, dy = panel_order(i)
        slot = dz * SIDE + dy
        panel = at(dz, dy)

        def arrived(axis):
            where = (axis, dz, dy)
            remote(
                right.at[where], right.at[where], pack_send.at[0, 0, 0], right_recv.at[where], along(axis, 1)
            ).wait_recv()

        @pl.when(dz > 0)
        def _():
            arrived(0)

        @pl.when(dy > 0)
        def _():
            arrived(1)

        for t in range(CAP):
            span = pl.ds(t * PORES, PORES)
            entry = jnp.concatenate([right[0, dz, dy, t], right[1, dz, dy, t]], axis=0)
            mid[span, :] = jnp.dot(amat[panel, t], entry, preferred_element_type=F32).astype(BF16)
            live = t < tabs_s[T_COUNT, panel]
            live = jnp.full((WIDTH, PORES), jnp.where(live, 1.0, 0.0), F32).astype(BF16)
            lt[:, span] = vt[tabs_s[T_ROWS + t, panel]] * live
        for e, target in ((0, give.at[0, slot]), (2, give.at[1, slot]), (1, own.at[slot])):
            target[...] = jnp.dot(
                lt[pl.ds(e * PORES, PORES), :], mid[...], preferred_element_type=F32
            ).astype(BF16)
        for copy in gives(slot):
            copy.start()

    def finish(i):
        dz, dy = panel_order(i)
        slot = dz * SIDE + dy
        panel = at(dz, dy)
        for copy in gives(slot):
            copy.wait()

        def block(ref, f):
            return ref[:, pl.ds(f * PORES, PORES)].astype(F32)

        for d in range(5):
            value = None
            for ref, f in ((own.at[slot], d - 1), (got.at[1, slot], d), (got.at[0, slot], d - 2)):
                if 0 <= f < 3:
                    term = block(ref, f)
                    value = term if value is None else value + term
            out[pl.ds(d * PANELS + panel, PORES, stride=5 * PANELS), :] = value

    def step(i, carry):
        product(i)

        @pl.when(i >= 2)
        def _():
            finish(i - 2)

        return carry

    lax.fori_loop(0, PANELS, step, 0)
    lax.fori_loop(PANELS - 2, PANELS, lambda i, carry: (finish(i), carry)[1], 0)

    for copy in sent:
        copy.wait_send()
    for copy in ring.values():
        copy.wait_send()


def per_device(fine_blocks, block_rows, block_cols, block_counts, prolong_blocks, prolong_mask):
    table = jnp.concatenate(
        [block_cols[0, 0].T, block_rows[0, 0].T, block_counts[0, 0][None], prolong_mask[0].T], axis=0
    )
    table = jnp.pad(table, ((0, T_ALL - table.shape[0]), (0, PORES - table.shape[1])))
    any_spec = pl.BlockSpec(memory_space=pl.ANY)
    vmem_spec = pl.BlockSpec(memory_space=pltpu.VMEM)
    half_rows = (ROWS, HALF, WIDTH)
    chunk = (CAP, HALF, WIDTH)
    dma = pltpu.SemaphoreType.DMA
    result = pl.pallas_call(
        kernel,
        out_shape=jax.ShapeDtypeStruct((PORES * 5 * PANELS, PORES), F32),
        in_specs=[any_spec, vmem_spec, any_spec],
        out_specs=vmem_spec,
        scratch_shapes=[
            pltpu.VMEM((ROWS, PORES, WIDTH), BF16),
            pltpu.VMEM((PANELS, CAP, PORES, PORES), BF16),
            pltpu.VMEM((ROWS, WIDTH, PORES), BF16),
            *[pltpu.VMEM(half_rows, BF16) for _ in range(8)],
            pltpu.VMEM((2, SIDE, SIDE) + chunk, BF16),
            pltpu.VMEM((2, 3, SIDE) + chunk, BF16),
            pltpu.VMEM((2, 2, 2) + chunk, BF16),
            pltpu.VMEM((6, CAP, PORES), jnp.int32),
            pltpu.SMEM((T_ALL, PORES), jnp.int32),
            pltpu.SMEM((6, CAP, PORES), jnp.int32),
            pltpu.VMEM((PANELS, PORES, WIDTH), BF16),
            pltpu.VMEM((2, PANELS, PORES, WIDTH), BF16),
            pltpu.VMEM((2, PANELS, PORES, WIDTH), BF16),
            pltpu.VMEM((WIDTH, CAP * PORES), BF16),
            pltpu.VMEM((CAP * PORES, WIDTH), BF16),
            dma((3,)),
            dma((6,)),
            dma((6,)),
            dma,
            dma((2, 6)),
            dma((2, 6)),
            dma((2, 3, SIDE)),
            dma((2, 2, 2)),
            dma((2, 2, 2)),
            dma((2, SIDE, SIDE)),
            dma((2, PANELS)),
            dma((2, PANELS)),
        ],
        compiler_params=pltpu.CompilerParams(
            collective_id=0, has_side_effects=True, vmem_limit_bytes=60 * 2**20
        ),
        cost_estimate=pl.CostEstimate(flops=6_500_000_000, bytes_accessed=12_000_000, transcendentals=0),
    )(fine_blocks[0, 0], table, prolong_blocks[0])
    coarse = result.reshape(PORES, 5, PANELS, PORES).transpose(0, 2, 1, 3)
    return coarse[None, None]


def solution(mesh):
    in_specs = (
        P("rows", "blk", None, None, None, None),
        P("rows", "blk", None, None),
        P("rows", "blk", None, None),
        P("rows", "blk", None),
        P("rows", "blk", None, None),
        P("rows", "blk", None),
    )
    out_specs = P("rows", "blk", None, None, None, None)
    return jax.shard_map(
        per_device, mesh=mesh, in_specs=in_specs, out_specs=out_specs, check_vma=False
    )
```

```python
import jax
import jax.numpy as jnp
from jax import lax
from jax.experimental import pallas as pl
from jax.experimental.pallas import tpu as pltpu
from jax.sharding import PartitionSpec as P

MESH = pl.DeviceIdType.MESH
BF16 = jnp.bfloat16
F32 = jnp.float32
SIDE = 4
ROWS = 16
CAP = 8
PORES = 128
HALF = 64
WIDTH = 384
GROUPS = 8
PANELS = 16
EARLY = 5
ORDER = (
    (0, 0), (0, 1), (1, 0), (0, 3), (3, 0),
    (0, 2), (2, 0), (1, 1), (1, 3), (3, 1), (3, 3), (2, 1), (1, 2), (2, 3), (3, 2), (2, 2),
)


def pick(values, i):
    n = len(values)
    total = values[0]
    for k in range(1, n):
        if values[k] != values[k - 1]:
            total = total + (values[k] - values[k - 1]) * ((i + n - k) // n)
    return total


def kernel(
    fine, prolong, cols_h, rows_h, counts_h, mask_h, out,
    stage, amat, vt, yg0, yg1, yg2, yg3, zg0, zg1, zg2, zg3,
    right, pack, tabs, cols, rows, counts, mask, near_s, own, give, got, lt, mid,
    load_sem, tab_send, tab_recv, tab_sem, ring_send, ring_recv, pack_send, right_recv, give_send, got_recv,
):
    blk, g = lax.axis_index("blk"), lax.axis_index("rows")
    z, y = blk // SIDE, blk % SIDE

    def at(dz, dy):
        return ((z + dz) % SIDE) * SIDE + (y + dy) % SIDE

    def along(axis, d):
        return (at(0, d), g) if axis == 0 else (at(d, 0), g)

    below, above = (blk, (g + GROUPS - 1) % GROUPS), (blk, (g + 1) % GROUPS)

    barrier = pltpu.get_barrier_semaphore()
    friends = [along(axis, d) for axis in range(2) for d in (1, 2, 3)] + [below, above]
    for friend in friends:
        pl.semaphore_signal(barrier, inc=1, device_id=friend, device_id_type=MESH)

    loads = [
        pltpu.make_async_copy(src, dst, load_sem.at[n])
        for n, (src, dst) in enumerate(
            ((prolong, stage), (mask_h, mask), (cols_h, cols), (rows_h, rows), (counts_h, counts), (fine, amat))
        )
    ]
    for load in loads:
        load.start()

    def remote(src, dst, send, recv, device):
        return pltpu.make_async_remote_copy(
            src_ref=src, dst_ref=dst, send_sem=send, recv_sem=recv, device_id=device, device_id_type=MESH
        )

    sent = []

    def send(*args):
        copy = remote(*args)
        copy.start()
        sent.append(copy)

    for load in loads[:2]:
        load.wait()

    def mask_row(j, carry):
        blocks = []
        for e in range(3):
            inside = jnp.logical_and(g + e - 1 >= 0, g + e - 1 < GROUPS)
            keep = jnp.logical_and(mask[e, 0, j] == 1, inside)
            keep = jnp.full((PORES, PORES), jnp.where(keep, 1.0, 0.0), F32).astype(BF16)
            blocks.append(stage[j, :, pl.ds(e * PORES, PORES)] * keep)
        row = jnp.concatenate(blocks, axis=1)
        yg0[j] = row[:HALF]
        zg0[j] = row[HALF:]
        return carry

    lax.fori_loop(0, ROWS, mask_row, 0)
    pl.semaphore_wait(barrier, len(friends))

    rings = ((yg0, yg1, yg2, yg3), (zg0, zg1, zg2, zg3))
    low, high = pl.ds(0, 8), pl.ds(8, 8)

    def ring_copy(axis, kind):
        r = rings[axis]
        up, down = along(axis, 1), along(axis, 3)
        src, dst, device = {
            0: (r[0].at[low], r[3].at[low], up),
            1: (r[0].at[high], r[1].at[high], down),
            2: (r[0].at[high], r[3].at[high], up),
            3: (r[0].at[low], r[1].at[low], down),
            4: (r[3].at[low], r[2].at[low], up),
            5: (r[1].at[high], r[2].at[high], down),
        }[kind]
        return remote(src, dst, ring_send.at[axis, kind], ring_recv.at[axis, kind], device)

    ring = {(axis, kind): ring_copy(axis, kind) for axis in range(2) for kind in range(6)}

    def tab_copy(axis, d, slot):
        return remote(cols_h, tabs.at[slot], tab_send.at[axis * 3 + d - 1], tab_recv.at[slot], along(axis, d))

    for axis in range(2):
        for d in (1, 2, 3):
            copy = tab_copy(axis, d, axis * 3 + (SIDE - d) - 1)
            copy.start()
            sent.append(copy)
    for kind in range(4):
        for axis in range(2):
            ring[axis, kind].start()

    def turn(j, carry):
        row = jnp.concatenate([yg0[j], zg0[j]], axis=0)
        vt[j] = row.T
        return carry

    for load in loads[2:5]:
        load.wait()
    for axis in range(2):
        for d in (1, 2, 3):
            tab_copy(axis, d, axis * 3 + d - 1).wait_recv()
    load_c = pltpu.make_async_copy(tabs, near_s, tab_sem)
    load_c.start()
    load_c.wait()

    def fill(dst, axis, d, who):
        src = rings[axis][d]
        panel = at(0, d) if axis == 0 else at(d, 0)

        def one(t, carry):
            column = cols[t, panel] if who is None else near_s[who, t, panel]
            dst[t] = src[column]
            return carry

        lax.fori_loop(0, CAP, one, 0)

    def place(axis, d, far):
        return (axis, far, d) if axis == 0 else (axis, d, far)

    def post(axis, d, t):
        other = 1 - axis
        slot = pack.at[axis, t - 1, d]
        fill(slot, axis, d, other * 3 + t - 1)
        where = place(axis, d, SIDE - t)
        send(slot, right.at[where], pack_send.at[axis, t - 1, d], right_recv.at[where], along(other, t))

    def post_all(d):
        for t in (1, 3, 2):
            for axis in range(2):
                post(axis, d, t)

    def keep(axis, d):
        fill(right.at[place(axis, d, 0)], axis, d, None)

    post_all(0)
    for kind in (0, 1):
        for axis in range(2):
            ring[axis, kind].wait_recv()
            ring[axis, kind + 4].start()
    lax.fori_loop(0, ROWS, turn, 0)
    for kind in (2, 3):
        for axis in range(2):
            ring[axis, kind].wait_recv()
    post_all(1)
    post_all(3)
    for d in (0, 1, 3):
        for axis in range(2):
            keep(axis, d)
    loads[5].wait()

    def gives(slot):
        return (
            remote(give.at[0, slot], got.at[0, slot], give_send.at[0, slot], got_recv.at[0, slot], below),
            remote(give.at[1, slot], got.at[1, slot], give_send.at[1, slot], got_recv.at[1, slot], above),
        )

    def offsets(i):
        dz, dy = pick([p[0] for p in ORDER], i), pick([p[1] for p in ORDER], i)
        return dz, dy, dz * SIDE + dy, at(dz, dy)

    def product(i):
        dz, dy, slot, panel = offsets(i)

        def arrived(axis):
            where = right.at[axis, dz, dy]
            remote(where, where, pack_send.at[0, 0, 0], right_recv.at[axis, dz, dy], along(axis, 1)).wait_recv()

        @pl.when(dz > 0)
        def _():
            arrived(0)

        @pl.when(dy > 0)
        def _():
            arrived(1)

        for t in range(CAP):
            span = pl.ds(t * PORES, PORES)
            entry = jnp.concatenate([right[0, dz, dy, t], right[1, dz, dy, t]], axis=0)
            mid[span, :] = jnp.dot(amat[panel, t], entry, preferred_element_type=F32).astype(BF16)
            live = t < counts[0, panel]
            live = jnp.full((WIDTH, PORES), jnp.where(live, 1.0, 0.0), F32).astype(BF16)
            lt[:, span] = vt[rows[t, panel]] * live
        below_copy, above_copy = gives(slot)
        for e, target in ((0, give.at[0, slot]), (2, give.at[1, slot]), (1, own.at[slot])):
            target[...] = jnp.dot(
                lt[pl.ds(e * PORES, PORES), :], mid[...], preferred_element_type=F32
            ).astype(BF16)
            if e == 0:
                below_copy.start()
            if e == 2:
                above_copy.start()

    def finish(i):
        dz, dy, slot, panel = offsets(i)
        for copy in gives(slot):
            copy.wait()

        def block(ref, f):
            return ref[:, pl.ds(f * PORES, PORES)].astype(F32)

        for d in range(5):
            value = None
            for ref, f in ((own.at[slot], d - 1), (got.at[1, slot], d), (got.at[0, slot], d - 2)):
                if 0 <= f < 3:
                    term = block(ref, f)
                    value = term if value is None else value + term
            out[pl.ds(d * PANELS + panel, PORES, stride=5 * PANELS), :] = value

    def step(i, carry):
        product(i)

        @pl.when(i >= 2)
        def _():
            finish(i - 2)

        return carry

    lax.fori_loop(0, EARLY, step, 0)
    for kind in (4, 5):
        for axis in range(2):
            ring[axis, kind].wait_recv()
    post_all(2)
    for axis in range(2):
        keep(axis, 2)
    lax.fori_loop(EARLY, PANELS, step, 0)
    lax.fori_loop(PANELS - 2, PANELS, lambda i, carry: (finish(i), carry)[1], 0)

    for copy in sent:
        copy.wait_send()
    for copy in ring.values():
        copy.wait_send()


def per_device(fine_blocks, block_rows, block_cols, block_counts, prolong_blocks, prolong_mask):
    any_spec = pl.BlockSpec(memory_space=pl.ANY)
    half_rows = (ROWS, HALF, WIDTH)
    chunk = (CAP, HALF, WIDTH)
    dma = pltpu.SemaphoreType.DMA
    result = pl.pallas_call(
        kernel,
        out_shape=pltpu.VMEM((PORES * 5 * PANELS, PORES), F32),
        in_specs=[any_spec] * 6,
        out_specs=pl.BlockSpec(memory_space=pltpu.VMEM),
        scratch_shapes=[
            pltpu.VMEM((ROWS, PORES, WIDTH), BF16),
            pltpu.VMEM((PANELS, CAP, PORES, PORES), BF16),
            pltpu.VMEM((ROWS, WIDTH, PORES), BF16),
            *[pltpu.VMEM(half_rows, BF16) for _ in range(8)],
            pltpu.VMEM((2, SIDE, SIDE) + chunk, BF16),
            pltpu.VMEM((2, 3, SIDE) + chunk, BF16),
            pltpu.VMEM((6, CAP, PANELS), jnp.int32),
            pltpu.SMEM((CAP, PANELS), jnp.int32),
            pltpu.SMEM((CAP, PANELS), jnp.int32),
            pltpu.SMEM((1, PANELS), jnp.int32),
            pltpu.SMEM((3, 1, ROWS), jnp.int32),
            pltpu.SMEM((6, CAP, PANELS), jnp.int32),
            pltpu.VMEM((PANELS, PORES, WIDTH), BF16),
            pltpu.VMEM((2, PANELS, PORES, WIDTH), BF16),
            pltpu.VMEM((2, PANELS, PORES, WIDTH), BF16),
            pltpu.VMEM((WIDTH, CAP * PORES), BF16),
            pltpu.VMEM((CAP * PORES, WIDTH), BF16),
            dma((6,)),
            dma((6,)),
            dma((6,)),
            dma,
            dma((2, 6)),
            dma((2, 6)),
            dma((2, 3, SIDE)),
            dma((2, SIDE, SIDE)),
            dma((2, PANELS)),
            dma((2, PANELS)),
        ],
        compiler_params=pltpu.CompilerParams(
            collective_id=0, has_side_effects=True, vmem_limit_bytes=50 * 2**20
        ),
        cost_estimate=pl.CostEstimate(flops=6_500_000_000, bytes_accessed=12_000_000, transcendentals=0),
    )(
        fine_blocks[0, 0],
        prolong_blocks[0],
        block_cols[0, 0].T,
        block_rows[0, 0].T,
        block_counts[0],
        prolong_mask.transpose(2, 0, 1),
    )
    coarse = result.reshape(PORES, 5, PANELS, PORES).transpose(0, 2, 1, 3)
    return coarse[None, None]


def solution(mesh):
    in_specs = (
        P("rows", "blk", None, None, None, None),
        P("rows", "blk", None, None),
        P("rows", "blk", None, None),
        P("rows", "blk", None),
        P("rows", "blk", None, None),
        P("rows", "blk", None),
    )
    out_specs = P("rows", "blk", None, None, None, None)
    return jax.shard_map(
        per_device, mesh=mesh, in_specs=in_specs, out_specs=out_specs, check_vma=False
    )
```

```python
import jax
import jax.numpy as jnp
from jax import lax
from jax.experimental import pallas as pl
from jax.experimental.pallas import tpu as pltpu
from jax.sharding import PartitionSpec as P

MESH = pl.DeviceIdType.MESH
BF16 = jnp.bfloat16
F32 = jnp.float32
SIDE = 4
ROWS = 16
CAP = 8
PORES = 128
WIDTH = 384
GROUPS = 8
PANELS = 16
OFFSETS = 5
T_ROWS, T_COUNT, T_ALL = 8, 16, 24
HELD = ((0, 0), (0, 1), (0, 3), (1, 0), (3, 0), (0, 2), (2, 0))
NEAR, LOCAL = 5, 7
SENT = (
    ((2, 2), (0, 2)), ((2, 1), (0, 1)), ((1, 3), (0, 3)), ((1, 1), (1, 0)), ((3, 3), (3, 0)),
    ((2, 3), (0, 3)), ((1, 2), (1, 0)), ((3, 1), (3, 0)), ((3, 2), (3, 0)),
)


def minus(p, q):
    return (p[0] - q[0]) % SIDE, (p[1] - q[1]) % SIDE


LISTER = tuple(HELD.index(minus((0, 0), h)) for _, h in SENT)
COLUMN = tuple(HELD.index(minus(p, h)) for p, h in SENT)


def pick(values, i):
    n = len(values)
    total = values[0]
    for k in range(1, n):
        if values[k] != values[k - 1]:
            total = total + (values[k] - values[k - 1]) * ((i + n - k) // n)
    return total


def kernel(
    fine, prolong, cols_h, rows_h, counts_h, mask_h, out,
    stage, amat, held, far, turned, tab, tabs, counts, mask, tabs_s,
    listed, own, give, got, result, returned, lt, mid,
    load_sem, tab_send, tab_recv, tab_sem, ring_send, ring_recv, list_send, list_recv, give_send, got_recv,
    result_send, result_recv,
):
    blk, g = lax.axis_index("blk"), lax.axis_index("rows")
    z, y = blk // SIDE, blk % SIDE

    def at(offset):
        dz, dy = offset
        return ((z + dz) % SIDE) * SIDE + (y + dy) % SIDE

    def device(offset):
        return at(offset), g

    below, above = (blk, (g + GROUPS - 1) % GROUPS), (blk, (g + 1) % GROUPS)

    barrier = pltpu.get_barrier_semaphore()
    friends = [device(offset) for offset in HELD[1:6]] + [below, above]
    for friend in friends:
        pl.semaphore_signal(barrier, inc=1, device_id=friend, device_id_type=MESH)

    loads = [
        pltpu.make_async_copy(src, dst, load_sem.at[n])
        for n, (src, dst) in enumerate(
            (
                (prolong, stage),
                (mask_h, mask),
                (cols_h, tab.at[pl.ds(0, CAP)]),
                (rows_h, tab.at[pl.ds(T_ROWS, CAP)]),
                (counts_h, counts),
                (fine, amat),
            )
        )
    ]
    for load in loads:
        load.start()

    def remote(src, dst, send, recv, target):
        return pltpu.make_async_remote_copy(
            src_ref=src, dst_ref=dst, send_sem=send, recv_sem=recv, device_id=target, device_id_type=MESH
        )

    for load in loads[:2]:
        load.wait()

    def mask_row(j, carry):
        for e in range(3):
            inside = jnp.logical_and(g + e - 1 >= 0, g + e - 1 < GROUPS)
            keep = jnp.logical_and(mask[e, 0, j] == 1, inside)
            keep = jnp.full((PORES, PORES), jnp.where(keep, 1.0, 0.0), F32).astype(BF16)
            span = pl.ds(e * PORES, PORES)
            held[0, j, :, span] = stage[j, :, span] * keep
        return carry

    lax.fori_loop(0, ROWS, mask_row, 0)
    for load in loads[2:5]:
        load.wait()
    tab[pl.ds(T_COUNT, CAP), :] = jnp.broadcast_to(counts[...], (CAP, PANELS))
    pl.semaphore_wait(barrier, len(friends))

    def tab_copy(n, target):
        return remote(tab, tabs.at[n], tab_send.at[n], tab_recv.at[n], target)

    for n in range(1, 6):
        tab_copy(n, device(minus((0, 0), HELD[n]))).start()

    low, high = pl.ds(0, 8), pl.ds(8, 8)

    def ring_copy(axis, kind):
        next_at, last_at = 1 + 2 * axis, 2 + 2 * axis
        up, down = device(HELD[next_at]), device(HELD[last_at])
        src, dst, target = {
            0: (held.at[0, low], held.at[last_at, low], up),
            1: (held.at[0, high], held.at[next_at, high], down),
            2: (held.at[0, high], held.at[last_at, high], up),
            3: (held.at[0, low], held.at[next_at, low], down),
            4: (held.at[last_at, low], far.at[axis, low], up),
            5: (held.at[next_at, high], far.at[axis, high], down),
        }[kind]
        return remote(src, dst, ring_send.at[axis, kind], ring_recv.at[axis, kind], target)

    ring = {(axis, kind): ring_copy(axis, kind) for axis in range(2) for kind in range(6)}
    for kind in range(4):
        for axis in range(2):
            ring[axis, kind].start()

    def turn(n):
        def one(j, carry):
            turned[n, j] = held[n, j].T
            return carry

        lax.fori_loop(0, ROWS, one, 0)

    turn(0)
    for n in range(1, 6):
        tab_copy(n, device(HELD[n])).wait_recv()
    copies = [
        pltpu.make_async_copy(tab, tabs_s.at[0], tab_sem.at[0]),
        pltpu.make_async_copy(tabs.at[pl.ds(1, 5)], tabs_s.at[pl.ds(1, 5)], tab_sem.at[1]),
    ]
    for copy in copies:
        copy.start()
    for copy in copies:
        copy.wait()
    loads[5].wait()

    for kind in (0, 1):
        for axis in range(2):
            ring[axis, kind].wait_recv()
            ring[axis, kind + 4].start()

    def list_copy(k):
        panel, worker = SENT[k]
        return remote(amat.at[at(panel)], listed.at[k], list_send.at[k], list_recv.at[k], device(worker))

    for k in range(len(SENT)):
        list_copy(k).start()
    for kind in (2, 3):
        for axis in range(2):
            ring[axis, kind].wait_recv()
    for n in range(1, NEAR):
        turn(n)

    def gives(slot):
        return (
            remote(give.at[0, slot], got.at[0, slot], give_send.at[0, slot], got_recv.at[0, slot], below),
            remote(give.at[1, slot], got.at[1, slot], give_send.at[1, slot], got_recv.at[1, slot], above),
        )

    def product(slot, blocks, lister, column, panel):
        for t in range(CAP):
            span = pl.ds(t * PORES, PORES)
            entry = held[column, tabs_s[lister, t, panel]]
            mid[span, :] = jnp.dot(blocks[t], entry, preferred_element_type=F32).astype(BF16)
            live = t < tabs_s[lister, T_COUNT, panel]
            live = jnp.full((WIDTH, PORES), jnp.where(live, 1.0, 0.0), F32).astype(BF16)
            lt[:, span] = turned[lister, tabs_s[lister, T_ROWS + t, panel]] * live
        below_copy, above_copy = gives(slot)
        for e, target in ((0, give.at[0, slot]), (2, give.at[1, slot]), (1, own.at[slot])):
            target[...] = jnp.dot(
                lt[pl.ds(e * PORES, PORES), :], mid[...], preferred_element_type=F32
            ).astype(BF16)
            if e == 0:
                below_copy.start()
            if e == 2:
                above_copy.start()

    def summed(slot):
        for copy in gives(slot):
            copy.wait()

        def block(ref, f):
            return ref[:, pl.ds(f * PORES, PORES)].astype(F32)

        values = []
        for d in range(OFFSETS):
            value = None
            for ref, f in ((own.at[slot], d - 1), (got.at[1, slot], d), (got.at[0, slot], d - 2)):
                if 0 <= f < 3:
                    term = block(ref, f)
                    value = term if value is None else value + term
            values.append(value)
        return values

    def store(values, panel):
        for d, value in enumerate(values):
            out[pl.ds(d * PANELS + panel, PORES, stride=OFFSETS * PANELS), :] = value

    def held_panel(i):
        return at((pick([p[0] for p in HELD], i), pick([p[1] for p in HELD], i)))

    def local_step(i, carry):
        panel = held_panel(i)
        product(i, amat.at[panel], 0, i, panel)

        @pl.when(i >= 2)
        def _():
            store(summed(i - 2), held_panel(i - 2))

        return carry

    def back(k):
        lister = (pick([HELD[n][0] for n in LISTER], k), pick([HELD[n][1] for n in LISTER], k))
        return remote(result.at[k], returned.at[k], result_send.at[k], result_recv.at[k], device(lister))

    def give_back(k):
        for d, value in enumerate(summed(k + LOCAL)):
            result[k, :, pl.ds(d * PORES, PORES)] = value.astype(BF16)
        back(k).start()

    def sent_step(k, carry):
        lister, column = pick(LISTER, k), pick(COLUMN, k)
        panel = held_panel(column)
        remote(listed.at[k], listed.at[k], list_send.at[k], list_recv.at[k], below).wait_recv()
        product(k + LOCAL, listed.at[k], lister, column, panel)

        @pl.when(k >= 2)
        def _():
            give_back(k - 2)

        return carry

    lax.fori_loop(0, NEAR, local_step, 0)
    for kind in (4, 5):
        for axis in range(2):
            ring[axis, kind].wait_recv()

    def settle(j, carry):
        for axis in range(2):
            held[NEAR + axis, j] = far[axis, j]
        return carry

    lax.fori_loop(0, ROWS, settle, 0)
    turn(NEAR)
    lax.fori_loop(NEAR, LOCAL, local_step, 0)
    for i in range(LOCAL - 2, LOCAL):
        store(summed(i), held_panel(i))
    last = len(SENT)
    lax.fori_loop(0, last, sent_step, 0)
    lax.fori_loop(last - 2, last, lambda k, carry: (give_back(k), carry)[1], 0)

    def arrive(k, carry):
        panel = at((pick([p[0] for p, _ in SENT], k), pick([p[1] for p, _ in SENT], k)))
        back(k).wait_recv()
        store([returned[k, :, pl.ds(d * PORES, PORES)].astype(F32) for d in range(OFFSETS)], panel)
        return carry

    lax.fori_loop(0, last, arrive, 0)

    for n in range(1, 6):
        tab_copy(n, device(minus((0, 0), HELD[n]))).wait_send()
    for copy in ring.values():
        copy.wait_send()
    for k in range(last):
        list_copy(k).wait_send()
        back(k).wait_send()


def per_device(fine_blocks, block_rows, block_cols, block_counts, prolong_blocks, prolong_mask):
    any_spec = pl.BlockSpec(memory_space=pl.ANY)
    dma = pltpu.SemaphoreType.DMA
    sent = len(SENT)
    value = pl.pallas_call(
        kernel,
        out_shape=pltpu.VMEM((PORES * OFFSETS * PANELS, PORES), F32),
        in_specs=[any_spec] * 6,
        out_specs=pl.BlockSpec(memory_space=pltpu.VMEM),
        scratch_shapes=[
            pltpu.VMEM((ROWS, PORES, WIDTH), BF16),
            pltpu.VMEM((PANELS, CAP, PORES, PORES), BF16),
            pltpu.VMEM((LOCAL, ROWS, PORES, WIDTH), BF16),
            pltpu.VMEM((2, ROWS, PORES, WIDTH), BF16),
            pltpu.VMEM((6, ROWS, WIDTH, PORES), BF16),
            pltpu.VMEM((T_ALL, PANELS), jnp.int32),
            pltpu.VMEM((6, T_ALL, PANELS), jnp.int32),
            pltpu.VMEM((1, PANELS), jnp.int32),
            pltpu.SMEM((3, 1, ROWS), jnp.int32),
            pltpu.SMEM((6, T_ALL, PANELS), jnp.int32),
            pltpu.VMEM((sent, CAP, PORES, PORES), BF16),
            pltpu.VMEM((PANELS, PORES, WIDTH), BF16),
            pltpu.VMEM((2, PANELS, PORES, WIDTH), BF16),
            pltpu.VMEM((2, PANELS, PORES, WIDTH), BF16),
            pltpu.VMEM((sent, PORES, OFFSETS * PORES), BF16),
            pltpu.VMEM((sent, PORES, OFFSETS * PORES), BF16),
            pltpu.VMEM((WIDTH, CAP * PORES), BF16),
            pltpu.VMEM((CAP * PORES, WIDTH), BF16),
            dma((6,)),
            dma((6,)),
            dma((6,)),
            dma((2,)),
            dma((2, 6)),
            dma((2, 6)),
            dma((sent,)),
            dma((sent,)),
            dma((2, PANELS)),
            dma((2, PANELS)),
            dma((sent,)),
            dma((sent,)),
        ],
        compiler_params=pltpu.CompilerParams(
            collective_id=0, has_side_effects=True, vmem_limit_bytes=52 * 2**20
        ),
        cost_estimate=pl.CostEstimate(flops=6_500_000_000, bytes_accessed=12_000_000, transcendentals=0),
    )(
        fine_blocks[0, 0],
        prolong_blocks[0],
        block_cols[0, 0].T,
        block_rows[0, 0].T,
        block_counts[0],
        prolong_mask.transpose(2, 0, 1),
    )
    coarse = value.reshape(PORES, OFFSETS, PANELS, PORES).transpose(0, 2, 1, 3)
    return coarse[None, None]


def solution(mesh):
    in_specs = (
        P("rows", "blk", None, None, None, None),
        P("rows", "blk", None, None),
        P("rows", "blk", None, None),
        P("rows", "blk", None),
        P("rows", "blk", None, None),
        P("rows", "blk", None),
    )
    out_specs = P("rows", "blk", None, None, None, None)
    return jax.shard_map(
        per_device, mesh=mesh, in_specs=in_specs, out_specs=out_specs, check_vma=False
    )
```

```python
import jax
import jax.numpy as jnp
from jax import lax
from jax.experimental import pallas as pl
from jax.experimental.pallas import tpu as pltpu
from jax.sharding import PartitionSpec as P

MESH = pl.DeviceIdType.MESH
BF16 = jnp.bfloat16
F32 = jnp.float32
SIDE = 4
ROWS = 16
CAP = 8
PORES = 128
WIDTH = 384
GROUPS = 8
PANELS = 16
OFFSETS = 5
T_ROWS, T_COUNT, T_ALL = 8, 16, 24
HELD = ((0, 0), (0, 1), (0, 3), (1, 0), (3, 0), (0, 2), (2, 0))
NEAR, LOCAL = 5, 7
SENT = (
    ((2, 2), (0, 2)),
    ((2, 1), (0, 1)), ((2, 3), (0, 3)), ((1, 2), (1, 0)), ((3, 2), (3, 0)),
    ((3, 1), (0, 1)), ((1, 3), (0, 3)), ((1, 1), (1, 0)), ((3, 3), (3, 0)),
)
ACROSS = 0


def minus(p, q):
    return (p[0] - q[0]) % SIDE, (p[1] - q[1]) % SIDE


LISTER = tuple(HELD.index(minus((0, 0), h)) for _, h in SENT)
COLUMN = tuple(HELD.index(minus(p, h)) for p, h in SENT)
IS_ACROSS = tuple(int(k == ACROSS) for k in range(len(SENT)))
STEPS = ((0, 1, 2, 3, 4), (7, 5, 6, 8, 9, 10, 11), (12, 13, 14, 15))
ORDER = sum(STEPS, ())
STARTS = tuple(sum(len(s) for s in STEPS[:n]) for n in range(len(STEPS) + 1))


def pick(values, i):
    if isinstance(i, int):
        return values[i]
    total = values[0]
    for k in range(1, len(values)):
        if values[k] != values[k - 1]:
            total = total + (values[k] - values[k - 1]) * (i >= k).astype(jnp.int32)
    return total


def kernel(
    fine, prolong, cols_h, rows_h, counts_h, mask_h, out,
    stage, blocks, held, far_y, far_z, turned, tab, tabs, counts, mask, tabs_s,
    own, give, got, result, returned, lt,
    load_sem, tab_send, tab_recv, tab_sem, ring_send, ring_recv, list_send, list_recv, give_send, got_recv,
    result_send, result_recv,
):
    blk, g = lax.axis_index("blk"), lax.axis_index("rows")
    z, y = blk // SIDE, blk % SIDE
    odd = (z + y) % 2
    across = (2 * odd, 2 * (1 - odd))

    def at(offset):
        dz, dy = offset
        return ((z + dz) % SIDE) * SIDE + (y + dy) % SIDE

    def device(offset):
        return at(offset), g

    below, above = (blk, (g + GROUPS - 1) % GROUPS), (blk, (g + 1) % GROUPS)

    barrier = pltpu.get_barrier_semaphore()
    friends = [device(offset) for offset in HELD[1:NEAR] + (across,)] + [below, above]
    for friend in friends:
        pl.semaphore_signal(barrier, inc=1, device_id=friend, device_id_type=MESH)

    loads = [
        pltpu.make_async_copy(src, dst, load_sem.at[n])
        for n, (src, dst) in enumerate(
            (
                (prolong, stage),
                (mask_h, mask),
                (cols_h, tab.at[pl.ds(0, CAP)]),
                (rows_h, tab.at[pl.ds(T_ROWS, CAP)]),
                (counts_h, counts),
                (fine, blocks.at[pl.ds(0, PANELS)]),
            )
        )
    ]
    for load in loads:
        load.start()

    def remote(src, dst, send, recv, target):
        return pltpu.make_async_remote_copy(
            src_ref=src, dst_ref=dst, send_sem=send, recv_sem=recv, device_id=target, device_id_type=MESH
        )

    for load in loads[:2]:
        load.wait()

    def mask_row(j, carry):
        for e in range(3):
            inside = jnp.logical_and(g + e - 1 >= 0, g + e - 1 < GROUPS)
            keep = jnp.logical_and(mask[e, 0, j] == 1, inside)
            keep = jnp.full((PORES, PORES), jnp.where(keep, 1.0, 0.0), F32).astype(BF16)
            span = pl.ds(e * PORES, PORES)
            held[0, j, :, span] = stage[j, :, span] * keep
        return carry

    lax.fori_loop(0, ROWS, mask_row, 0)
    for load in loads[2:5]:
        load.wait()
    tab[pl.ds(T_COUNT, CAP), :] = jnp.broadcast_to(counts[...], (CAP, PANELS))
    pl.semaphore_wait(barrier, len(friends))

    def tab_copy(n, target):
        return remote(tab, tabs.at[n], tab_send.at[n], tab_recv.at[n], target)

    tab_targets = [minus((0, 0), HELD[n]) for n in range(1, NEAR)] + [across]
    for n in range(1, 6):
        tab_copy(n, device(tab_targets[n - 1])).start()

    low, high = pl.ds(0, 8), pl.ds(8, 8)

    def ring_copy(axis, kind):
        next_at, last_at = 1 + 2 * axis, 2 + 2 * axis
        up, down = device(HELD[next_at]), device(HELD[last_at])
        far = (far_y, far_z)[axis]
        src, dst, target = {
            0: (held.at[0, low], held.at[last_at, low], up),
            1: (held.at[0, high], held.at[next_at, high], down),
            2: (held.at[0, high], held.at[last_at, high], up),
            3: (held.at[0, low], held.at[next_at, low], down),
            4: (held.at[last_at, low], far.at[low], up),
            5: (held.at[next_at, high], far.at[high], down),
        }[kind]
        return remote(src, dst, ring_send.at[axis, kind], ring_recv.at[axis, kind], target)

    ring = {(axis, kind): ring_copy(axis, kind) for axis in range(2) for kind in range(6)}
    for kind in range(4):
        for axis in range(2):
            ring[axis, kind].start()

    def turn(n, source, first=0, last=ROWS):
        def one(j, carry):
            turned[n, j] = held[source, j].T
            return carry

        lax.fori_loop(first, last, one, 0)

    loads[5].wait()

    def list_copy(k):
        panel, worker = SENT[k]
        worker = across if k == ACROSS else worker
        return remote(blocks.at[at(panel)], blocks.at[PANELS + k], list_send.at[k], list_recv.at[k], device(worker))

    list_copy(ACROSS).start()
    turn(0, 0)
    for n in range(1, 6):
        tab_copy(n, device(tab_targets[n - 1])).wait_recv()
    copies = [
        pltpu.make_async_copy(tab, tabs_s.at[0], tab_sem.at[0]),
        pltpu.make_async_copy(tabs.at[pl.ds(1, 5)], tabs_s.at[pl.ds(1, 5)], tab_sem.at[1]),
    ]
    for copy in copies:
        copy.start()
    for copy in copies:
        copy.wait()

    for kind in (0, 1):
        for axis in range(2):
            ring[axis, kind].wait_recv()
            ring[axis, kind + 4].start()
    for k in range(ACROSS + 1, len(SENT)):
        list_copy(k).start()
    for n, first in ((2, 0), (4, 0), (1, 8), (3, 8)):
        turn(n, n, first, first + 8)
    for kind in (2, 3):
        for axis in range(2):
            ring[axis, kind].wait_recv()
    for n, first in ((2, 8), (4, 8), (1, 0), (3, 0)):
        turn(n, n, first, first + 8)

    def gives(slot):
        return (
            remote(give.at[0, slot], got.at[0, slot], give_send.at[0, slot], got_recv.at[0, slot], below),
            remote(give.at[1, slot], got.at[1, slot], give_send.at[1, slot], got_recv.at[1, slot], above),
        )

    def product(slot, at_block, lister, column, panel):
        entries = []
        for t in range(CAP):
            live = jnp.where(t < tabs_s[lister, T_COUNT, panel], 1.0, 0.0)
            block = blocks[at_block, t] * jnp.full((PORES, PORES), live, F32).astype(BF16)
            row = turned[lister, tabs_s[lister, T_ROWS + t, panel]]
            lt[:, pl.ds(t * PORES, PORES)] = jnp.dot(row, block, preferred_element_type=F32).astype(BF16)
            entries.append(held[column, tabs_s[lister, t, panel]])
        total = jnp.dot(lt[...], jnp.concatenate(entries, axis=0), preferred_element_type=F32).astype(BF16)
        give[0, slot] = total[:PORES]
        give[1, slot] = total[2 * PORES :]
        own[slot] = total[PORES : 2 * PORES]
        for copy in gives(slot):
            copy.start()

    def summed(slot):
        for copy in gives(slot):
            copy.wait()

        def block(ref, f):
            return ref[:, pl.ds(f * PORES, PORES)].astype(F32)

        values = []
        for d in range(OFFSETS):
            value = None
            for ref, f in ((own.at[slot], d - 1), (got.at[1, slot], d), (got.at[0, slot], d - 2)):
                if 0 <= f < 3:
                    term = block(ref, f)
                    value = term if value is None else value + term
            values.append(value)
        return values

    def store(values, panel):
        for d, value in enumerate(values):
            out[pl.ds(d * PANELS + panel, PORES, stride=OFFSETS * PANELS), :] = value

    def held_panel(i):
        return at((pick([p[0] for p in HELD], i), pick([p[1] for p in HELD], i)))

    def back(k):
        far_one = pick(IS_ACROSS, k)
        lister = tuple(
            pick([HELD[n][axis] * (1 - a) for n, a in zip(LISTER, IS_ACROSS)], k) + far_one * across[axis]
            for axis in range(2)
        )
        return remote(result.at[k], returned.at[k], result_send.at[k], result_recv.at[k], device(lister))

    def give_back(k, slot):
        for d, value in enumerate(summed(slot)):
            result[k, :, pl.ds(d * PORES, PORES)] = value.astype(BF16)
        back(k).start()

    def settle(axis):
        for kind in (4, 5):
            ring[axis, kind].wait_recv()
        source = (far_y, far_z)[axis]

        def one(j, carry):
            held[NEAR + axis, j] = source[j]
            return carry

        lax.fori_loop(0, ROWS, one, 0)

    def work(i, carry):
        step = pick(ORDER, i)
        here = pick([int(n < LOCAL) for n in ORDER], i)
        k = (step - LOCAL) * (1 - here)
        lister = pick(LISTER, k) * (1 - here)
        column = step * here + (pick(COLUMN, k) - odd * pick(IS_ACROSS, k)) * (1 - here)
        panel = held_panel(column)

        @pl.when(here == 0)
        def _():
            remote(blocks.at[PANELS + k], blocks.at[PANELS + k], list_send.at[k], list_recv.at[k], below).wait_recv()

        product(i, panel * here + (PANELS + k) * (1 - here), lister, column, panel)
        return carry

    def finish(i, carry):
        step = pick(ORDER, i)

        @pl.when(step < LOCAL)
        def _():
            store(summed(i), held_panel(step))

        @pl.when(step >= LOCAL)
        def _():
            give_back(step - LOCAL, i)

        return carry

    def stretch(n, carry):
        @pl.when(n == 1)
        def _():
            settle(0)
            settle(1)
            turn(NEAR, NEAR + odd)

        first, last = pick(STARTS, n), pick(STARTS, n + 1)
        lax.fori_loop(first, last, work, 0)
        lax.fori_loop(first, last, finish, 0)
        return carry

    lax.fori_loop(0, len(STEPS), stretch, 0)

    last = len(SENT)

    def arrive(k, carry):
        panel = at((pick([p[0] for p, _ in SENT], k), pick([p[1] for p, _ in SENT], k)))
        back(k).wait_recv()
        store([returned[k, :, pl.ds(d * PORES, PORES)].astype(F32) for d in range(OFFSETS)], panel)
        return carry

    lax.fori_loop(0, last, arrive, 0)

    for n in range(1, 6):
        tab_copy(n, device(tab_targets[n - 1])).wait_send()
    for copy in ring.values():
        copy.wait_send()
    for k in range(last):
        list_copy(k).wait_send()
        back(k).wait_send()


def per_device(fine_blocks, block_rows, block_cols, block_counts, prolong_blocks, prolong_mask):
    any_spec = pl.BlockSpec(memory_space=pl.ANY)
    dma = pltpu.SemaphoreType.DMA
    sent = len(SENT)
    value = pl.pallas_call(
        kernel,
        out_shape=pltpu.VMEM((PORES * OFFSETS * PANELS, PORES), F32),
        in_specs=[any_spec] * 6,
        out_specs=pl.BlockSpec(memory_space=pltpu.VMEM),
        scratch_shapes=[
            pltpu.VMEM((ROWS, PORES, WIDTH), BF16),
            pltpu.VMEM((PANELS + sent, CAP, PORES, PORES), BF16),
            pltpu.VMEM((LOCAL, ROWS, PORES, WIDTH), BF16),
            pltpu.VMEM((ROWS, PORES, WIDTH), BF16),
            pltpu.VMEM((ROWS, PORES, WIDTH), BF16),
            pltpu.VMEM((6, ROWS, WIDTH, PORES), BF16),
            pltpu.VMEM((T_ALL, PANELS), jnp.int32),
            pltpu.VMEM((6, T_ALL, PANELS), jnp.int32),
            pltpu.VMEM((1, PANELS), jnp.int32),
            pltpu.SMEM((3, 1, ROWS), jnp.int32),
            pltpu.SMEM((6, T_ALL, PANELS), jnp.int32),
            pltpu.VMEM((PANELS, PORES, WIDTH), BF16),
            pltpu.VMEM((2, PANELS, PORES, WIDTH), BF16),
            pltpu.VMEM((2, PANELS, PORES, WIDTH), BF16),
            pltpu.VMEM((sent, PORES, OFFSETS * PORES), BF16),
            pltpu.VMEM((sent, PORES, OFFSETS * PORES), BF16),
            pltpu.VMEM((WIDTH, CAP * PORES), BF16),
            dma((6,)),
            dma((6,)),
            dma((6,)),
            dma((2,)),
            dma((2, 6)),
            dma((2, 6)),
            dma((sent,)),
            dma((sent,)),
            dma((2, PANELS)),
            dma((2, PANELS)),
            dma((sent,)),
            dma((sent,)),
        ],
        compiler_params=pltpu.CompilerParams(
            collective_id=0, has_side_effects=True, vmem_limit_bytes=52 * 2**20
        ),
        cost_estimate=pl.CostEstimate(flops=6_500_000_000, bytes_accessed=12_000_000, transcendentals=0),
    )(
        fine_blocks[0, 0],
        prolong_blocks[0],
        block_cols[0, 0].T,
        block_rows[0, 0].T,
        block_counts[0],
        prolong_mask.transpose(2, 0, 1),
    )
    coarse = value.reshape(PORES, OFFSETS, PANELS, PORES).transpose(0, 2, 1, 3)
    return coarse[None, None]


def solution(mesh):
    in_specs = (
        P("rows", "blk", None, None, None, None),
        P("rows", "blk", None, None),
        P("rows", "blk", None, None),
        P("rows", "blk", None),
        P("rows", "blk", None, None),
        P("rows", "blk", None),
    )
    out_specs = P("rows", "blk", None, None, None, None)
    return jax.shard_map(
        per_device, mesh=mesh, in_specs=in_specs, out_specs=out_specs, check_vma=False
    )
```

```python
import jax
import jax.numpy as jnp
from jax import lax
from jax.experimental import pallas as pl
from jax.experimental.pallas import tpu as pltpu
from jax.sharding import PartitionSpec as P

MESH = pl.DeviceIdType.MESH
BF16 = jnp.bfloat16
F32 = jnp.float32
SIDE = 4
ROWS = 16
CAP = 8
PORES = 128
WIDTH = 384
GROUPS = 8
PANELS = 16
OFFSETS = 5
T_ROWS, T_COUNT, T_ALL = 8, 16, 24
HELD = ((0, 0), (0, 1), (0, 3), (1, 0), (3, 0), (0, 2), (2, 0))
NEAR, LOCAL = 5, 7
SENT = (
    ((2, 2), (0, 2)), ((1, 1), (1, 0)), ((3, 3), (3, 0)),
    ((2, 1), (0, 1)), ((2, 3), (0, 3)), ((1, 2), (1, 0)), ((3, 2), (3, 0)),
    ((1, 3), (0, 3)), ((3, 1), (3, 0)),
)
FIRST = 3


def minus(p, q):
    return (p[0] - q[0]) % SIDE, (p[1] - q[1]) % SIDE


LISTER = tuple(HELD.index(minus((0, 0), h)) for _, h in SENT)
COLUMN = tuple(HELD.index(minus(p, h)) for p, h in SENT)
PRODUCT, SUM, RETURN, TURN = range(4)
ORDER = (
    *((PRODUCT, i) for i in (0, 1, 2, 3, 4, 8, 9)),
    *((SUM, i) for i in (0, 1, 2, 3, 4, 8, 9)),
    (PRODUCT, 5), (PRODUCT, 6), (TURN, 5), (PRODUCT, 7),
    *((PRODUCT, i) for i in (10, 11, 12, 13)),
    *((SUM, i) for i in (7, 5, 6, 10, 11)),
    (PRODUCT, 14), (PRODUCT, 15),
    *((SUM, i) for i in (12, 13, 14, 15)),
    *((RETURN, k) for k in (1, 2, 0, 3, 4, 5, 6, 7, 8)),
)
FAR_OP = ORDER.index((PRODUCT, 5))


def pick(values, i):
    if isinstance(i, int):
        return values[i]
    words = []
    for first in range(0, len(values), 8):
        word = sum(value << (4 * n) for n, value in enumerate(values[first : first + 8]))
        words.append(word - (1 << 32) if word >= 1 << 31 else word)
    chosen = jnp.int32(words[-1])
    for n in range(len(words) - 2, -1, -1):
        chosen = jnp.where(i < 8 * (n + 1), jnp.int32(words[n]), chosen)
    return lax.shift_right_logical(chosen, (i & 7) * 4) & 15


def kernel(
    fine, prolong, cols_h, rows_h, counts_h, mask_h, out,
    stage, blocks, held, far, turned, tab, tabs, counts, mask, tabs_s,
    own, give, got, result, returned, mid,
    load_sem, tab_send, tab_recv, tab_sem, ring_send, ring_recv, list_send, list_recv, give_send, got_recv,
    result_send, result_recv,
):
    blk, g = lax.axis_index("blk"), lax.axis_index("rows")
    z, y = blk // SIDE, blk % SIDE

    def at(offset):
        dz, dy = offset
        return ((z + dz) % SIDE) * SIDE + (y + dy) % SIDE

    def device(offset):
        return at(offset), g

    below, above = (blk, (g + GROUPS - 1) % GROUPS), (blk, (g + 1) % GROUPS)

    barrier = pltpu.get_barrier_semaphore()
    friends = [device(offset) for offset in HELD[1:6]] + [below, above]
    for friend in friends:
        pl.semaphore_signal(barrier, inc=1, device_id=friend, device_id_type=MESH)

    loads = [
        pltpu.make_async_copy(src, dst, load_sem.at[n])
        for n, (src, dst) in enumerate(
            (
                (prolong, stage),
                (mask_h, mask),
                (cols_h, tab.at[pl.ds(0, CAP)]),
                (rows_h, tab.at[pl.ds(T_ROWS, CAP)]),
                (counts_h, counts),
                (fine, blocks.at[pl.ds(0, PANELS)]),
            )
        )
    ]
    for load in loads:
        load.start()

    def remote(src, dst, send, recv, target):
        return pltpu.make_async_remote_copy(
            src_ref=src, dst_ref=dst, send_sem=send, recv_sem=recv, device_id=target, device_id_type=MESH
        )

    for load in loads[:2]:
        load.wait()

    def mask_row(j, carry):
        for e in range(3):
            inside = jnp.logical_and(g + e - 1 >= 0, g + e - 1 < GROUPS)
            keep = jnp.logical_and(mask[e, 0, j] == 1, inside)
            keep = jnp.full((PORES, PORES), jnp.where(keep, 1.0, 0.0), F32).astype(BF16)
            span = pl.ds(e * PORES, PORES)
            held[0, j, :, span] = stage[j, :, span] * keep
        return carry

    lax.fori_loop(0, ROWS, mask_row, 0)
    for load in loads[2:5]:
        load.wait()
    tab[pl.ds(T_COUNT, CAP), :] = jnp.broadcast_to(counts[...], (CAP, PANELS))
    pl.semaphore_wait(barrier, len(friends))

    def tab_copy(n, target):
        return remote(tab, tabs.at[n], tab_send.at[n], tab_recv.at[n], target)

    tab_targets = [minus((0, 0), HELD[n]) for n in range(1, 6)]
    for n in range(1, 6):
        tab_copy(n, device(tab_targets[n - 1])).start()

    low, high = pl.ds(0, 8), pl.ds(8, 8)

    def ring_copy(axis, kind):
        next_at, last_at = 1 + 2 * axis, 2 + 2 * axis
        up, down = device(HELD[next_at]), device(HELD[last_at])
        src, dst, target = {
            0: (held.at[0, low], held.at[last_at, low], up),
            1: (held.at[0, high], held.at[next_at, high], down),
            2: (held.at[0, high], held.at[last_at, high], up),
            3: (held.at[0, low], held.at[next_at, low], down),
            4: (held.at[last_at, low], far.at[axis, low], up),
            5: (held.at[next_at, high], far.at[axis, high], down),
        }[kind]
        return remote(src, dst, ring_send.at[axis, kind], ring_recv.at[axis, kind], target)

    ring = {(axis, kind): ring_copy(axis, kind) for axis in range(2) for kind in range(6)}
    for kind in range(4):
        for axis in range(2):
            ring[axis, kind].start()

    def turn(n, first=0, last=ROWS):
        def one(j, carry):
            turned[n, j] = (held[n, j] if n < NEAR else far[n - NEAR, j]).T
            return carry

        lax.fori_loop(first, last, one, 0)

    loads[5].wait()

    def list_copy(k):
        panel, worker = SENT[k]
        return remote(blocks.at[at(panel)], blocks.at[PANELS + k], list_send.at[k], list_recv.at[k], device(worker))

    for k in range(FIRST):
        list_copy(k).start()
    turn(0)
    for n in range(1, 6):
        tab_copy(n, device(tab_targets[n - 1])).wait_recv()
    copies = [
        pltpu.make_async_copy(tab, tabs_s.at[0], tab_sem.at[0]),
        pltpu.make_async_copy(tabs.at[pl.ds(1, 5)], tabs_s.at[pl.ds(1, 5)], tab_sem.at[1]),
    ]
    for copy in copies:
        copy.start()
    for copy in copies:
        copy.wait()

    for kind in (0, 1):
        for axis in range(2):
            ring[axis, kind].wait_recv()
            ring[axis, kind + 4].start()
    for k in range(FIRST, len(SENT)):
        list_copy(k).start()
    for n, first in ((2, 0), (4, 0), (1, 8), (3, 8)):
        turn(n, first, first + 8)
    for kind in (2, 3):
        for axis in range(2):
            ring[axis, kind].wait_recv()
    for n, first in ((2, 8), (4, 8), (1, 0), (3, 0)):
        turn(n, first, first + 8)

    def gives(slot):
        return (
            remote(give.at[0, slot], got.at[0, slot], give_send.at[0, slot], got_recv.at[0, slot], below),
            remote(give.at[1, slot], got.at[1, slot], give_send.at[1, slot], got_recv.at[1, slot], above),
        )

    def product(source, slot, at_block, lister, column, panel):
        rows = []
        for t in range(CAP):
            live = jnp.where(t < tabs_s[lister, T_COUNT, panel], 1.0, 0.0)
            block = blocks[at_block, t] * jnp.full((PORES, PORES), live, F32).astype(BF16)
            entry = source[column, tabs_s[lister, t, panel]]
            mid[pl.ds(t * PORES, PORES), :] = jnp.dot(block, entry, preferred_element_type=F32).astype(BF16)
            rows.append(turned[lister, tabs_s[lister, T_ROWS + t, panel]])
        total = jnp.dot(jnp.concatenate(rows, axis=1), mid[...], preferred_element_type=F32).astype(BF16)
        give[0, slot] = total[:PORES]
        give[1, slot] = total[2 * PORES :]
        own[slot] = total[PORES : 2 * PORES]
        for copy in gives(slot):
            copy.start()

    def summed(slot):
        for copy in gives(slot):
            copy.wait()

        def block(ref, f):
            return ref[:, pl.ds(f * PORES, PORES)].astype(F32)

        values = []
        for d in range(OFFSETS):
            value = None
            for ref, f in ((own.at[slot], d - 1), (got.at[1, slot], d), (got.at[0, slot], d - 2)):
                if 0 <= f < 3:
                    term = block(ref, f)
                    value = term if value is None else value + term
            values.append(value)
        return values

    def store(values, panel):
        for d, value in enumerate(values):
            out[pl.ds(d * PANELS + panel, PORES, stride=OFFSETS * PANELS), :] = value

    def held_panel(i):
        return at((pick([p[0] for p in HELD], i), pick([p[1] for p in HELD], i)))

    def back(k):
        lister = (pick([HELD[n][0] for n in LISTER], k), pick([HELD[n][1] for n in LISTER], k))
        return remote(result.at[k], returned.at[k], result_send.at[k], result_recv.at[k], device(lister))

    def give_back(k, slot):
        for d, value in enumerate(summed(slot)):
            result[k, :, pl.ds(d * PORES, PORES)] = value.astype(BF16)
        back(k).start()

    def work(i):
        here = (i < LOCAL).astype(jnp.int32)
        k = (i - LOCAL) * (1 - here)
        lister = pick(LISTER, k) * (1 - here)
        column = i * here + pick(COLUMN, k) * (1 - here)
        panel = held_panel(column)
        at_block = panel * here + (PANELS + k) * (1 - here)

        @pl.when(here == 0)
        def _():
            remote(blocks.at[PANELS + k], blocks.at[PANELS + k], list_send.at[k], list_recv.at[k], below).wait_recv()

        @pl.when(column < NEAR)
        def _():
            product(held, i, at_block, lister, column, panel)

        @pl.when(column >= NEAR)
        def _():
            product(far, i, at_block, lister, column - NEAR, panel)

    def finish(i):
        @pl.when(i < LOCAL)
        def _():
            store(summed(i), held_panel(i))

        @pl.when(i >= LOCAL)
        def _():
            give_back(i - LOCAL, i)

    def arrive(k):
        panel = at((pick([p[0] for p, _ in SENT], k), pick([p[1] for p, _ in SENT], k)))
        back(k).wait_recv()
        store([returned[k, :, pl.ds(d * PORES, PORES)].astype(F32) for d in range(OFFSETS)], panel)

    def operate(n, carry):
        kind, i = pick([op for op, _ in ORDER], n), pick([i for _, i in ORDER], n)

        @pl.when(kind == PRODUCT)
        def _():
            work(i)

        @pl.when(kind == SUM)
        def _():
            finish(i)

        @pl.when(kind == RETURN)
        def _():
            arrive(i)

        @pl.when(kind == TURN)
        def _():
            turn(NEAR)

        return carry

    lax.fori_loop(0, FAR_OP, operate, 0)
    for kind in (4, 5):
        for axis in range(2):
            ring[axis, kind].wait_recv()
    lax.fori_loop(FAR_OP, len(ORDER), operate, 0)

    last = len(SENT)

    for n in range(1, 6):
        tab_copy(n, device(tab_targets[n - 1])).wait_send()
    for copy in ring.values():
        copy.wait_send()
    for k in range(last):
        list_copy(k).wait_send()
        back(k).wait_send()


def per_device(fine_blocks, block_rows, block_cols, block_counts, prolong_blocks, prolong_mask):
    any_spec = pl.BlockSpec(memory_space=pl.ANY)
    dma = pltpu.SemaphoreType.DMA
    sent = len(SENT)
    value = pl.pallas_call(
        kernel,
        out_shape=pltpu.VMEM((PORES * OFFSETS * PANELS, PORES), F32),
        in_specs=[any_spec] * 6,
        out_specs=pl.BlockSpec(memory_space=pltpu.VMEM),
        scratch_shapes=[
            pltpu.VMEM((ROWS, PORES, WIDTH), BF16),
            pltpu.VMEM((PANELS + sent, CAP, PORES, PORES), BF16),
            pltpu.VMEM((NEAR, ROWS, PORES, WIDTH), BF16),
            pltpu.VMEM((2, ROWS, PORES, WIDTH), BF16),
            pltpu.VMEM((6, ROWS, WIDTH, PORES), BF16),
            pltpu.VMEM((T_ALL, PANELS), jnp.int32),
            pltpu.VMEM((6, T_ALL, PANELS), jnp.int32),
            pltpu.VMEM((1, PANELS), jnp.int32),
            pltpu.SMEM((3, 1, ROWS), jnp.int32),
            pltpu.SMEM((6, T_ALL, PANELS), jnp.int32),
            pltpu.VMEM((PANELS, PORES, WIDTH), BF16),
            pltpu.VMEM((2, PANELS, PORES, WIDTH), BF16),
            pltpu.VMEM((2, PANELS, PORES, WIDTH), BF16),
            pltpu.VMEM((sent, PORES, OFFSETS * PORES), BF16),
            pltpu.VMEM((sent, PORES, OFFSETS * PORES), BF16),
            pltpu.VMEM((CAP * PORES, WIDTH), BF16),
            dma((6,)),
            dma((6,)),
            dma((6,)),
            dma((2,)),
            dma((2, 6)),
            dma((2, 6)),
            dma((sent,)),
            dma((sent,)),
            dma((2, PANELS)),
            dma((2, PANELS)),
            dma((sent,)),
            dma((sent,)),
        ],
        compiler_params=pltpu.CompilerParams(
            collective_id=0, has_side_effects=True, vmem_limit_bytes=52 * 2**20
        ),
        cost_estimate=pl.CostEstimate(flops=6_500_000_000, bytes_accessed=12_000_000, transcendentals=0),
    )(
        fine_blocks[0, 0],
        prolong_blocks[0],
        block_cols[0, 0].T,
        block_rows[0, 0].T,
        block_counts[0],
        prolong_mask.transpose(2, 0, 1),
    )
    coarse = value.reshape(PORES, OFFSETS, PANELS, PORES).transpose(0, 2, 1, 3)
    return coarse[None, None]


def solution(mesh):
    in_specs = (
        P("rows", "blk", None, None, None, None),
        P("rows", "blk", None, None),
        P("rows", "blk", None, None),
        P("rows", "blk", None),
        P("rows", "blk", None, None),
        P("rows", "blk", None),
    )
    out_specs = P("rows", "blk", None, None, None, None)
    return jax.shard_map(
        per_device, mesh=mesh, in_specs=in_specs, out_specs=out_specs, check_vma=False
    )
```

```python
import jax
import jax.numpy as jnp
from jax import lax
from jax.experimental import pallas as pl
from jax.experimental.pallas import tpu as pltpu
from jax.sharding import PartitionSpec as P

MESH = pl.DeviceIdType.MESH
BF16 = jnp.bfloat16
F32 = jnp.float32
SIDE = 4
ROWS = 16
UP = (10, 9)
CAP = 8
PORES = 128
WIDTH = 384
GROUPS = 8
PANELS = 16
OFFSETS = 5
T_ROWS, T_COUNT, T_ALL = 8, 16, 24
HELD = ((0, 0), (0, 1), (0, 3), (1, 0), (3, 0), (0, 2), (2, 0))
NEAR, LOCAL = 5, 7
SENT = (
    ((2, 2), (0, 2)),
    ((1, 1), (1, 0)),
    ((3, 3), (3, 0)),
    ((1, 3), (0, 3)),
    ((3, 1), (3, 0)),
    ((2, 1), (0, 1)),
    ((2, 3), (0, 3)),
    ((1, 2), (1, 0)),
    ((3, 2), (3, 0)),
)
FIRST = 5


def minus(p, q):
    return (p[0] - q[0]) % SIDE, (p[1] - q[1]) % SIDE


LISTER = tuple(HELD.index(minus((0, 0), h)) for _, h in SENT)
COLUMN = tuple(HELD.index(minus(p, h)) for p, h in SENT)
PRODUCT, SUM, RETURN, TURN = range(4)
ORDER = (
    (PRODUCT, 0),
    (PRODUCT, 1),
    (PRODUCT, 2),
    (PRODUCT, 3),
    (PRODUCT, 4),
    (PRODUCT, 8),
    (PRODUCT, 9),
    (PRODUCT, 10),
    (PRODUCT, 11),
    (SUM, 0),
    (SUM, 1),
    (SUM, 2),
    (SUM, 3),
    (SUM, 4),
    (SUM, 8),
    (SUM, 9),
    (SUM, 10),
    (SUM, 11),
    (PRODUCT, 5),
    (TURN, 5),
    (PRODUCT, 7),
    (PRODUCT, 6),
    (PRODUCT, 13),
    (PRODUCT, 15),
    (PRODUCT, 12),
    (PRODUCT, 14),
    (SUM, 7),
    (SUM, 5),
    (SUM, 6),
    (SUM, 13),
    (SUM, 15),
    (SUM, 12),
    (SUM, 14),
    *((RETURN, k) for k in (0, 1, 2, 3, 4, 6, 8, 5, 7)),
)
FAR_OP = ORDER.index((PRODUCT, 5))


def pick(values, i):
    if isinstance(i, int):
        return values[i]
    words = []
    for first in range(0, len(values), 8):
        word = sum(value << (4 * n) for n, value in enumerate(values[first : first + 8]))
        words.append(word - (1 << 32) if word >= 1 << 31 else word)
    chosen = jnp.int32(words[-1])
    for n in range(len(words) - 2, -1, -1):
        chosen = jnp.where(i < 8 * (n + 1), jnp.int32(words[n]), chosen)
    return lax.shift_right_logical(chosen, (i & 7) * 4) & 15


def kernel(
    fine, prolong, cols_h, rows_h, counts_h, mask_h, out,
    stage, blocks, held, far, turned, tab, tabs, counts, mask, tabs_s,
    own, give, got, result, returned, mid,
    load_sem, tab_send, tab_recv, tab_sem, ring_send, ring_recv, list_send, list_recv, give_send, got_recv,
    result_send, result_recv,
):
    blk, g = lax.axis_index("blk"), lax.axis_index("rows")
    z, y = blk // SIDE, blk % SIDE

    def at(offset):
        dz, dy = offset
        return ((z + dz) % SIDE) * SIDE + (y + dy) % SIDE

    def device(offset):
        return at(offset), g

    below, above = (blk, (g + GROUPS - 1) % GROUPS), (blk, (g + 1) % GROUPS)

    barrier = pltpu.get_barrier_semaphore()
    friends = [device(offset) for offset in HELD[1:6]] + [below, above]
    for friend in friends:
        pl.semaphore_signal(barrier, inc=1, device_id=friend, device_id_type=MESH)

    loads = [
        pltpu.make_async_copy(src, dst, load_sem.at[n])
        for n, (src, dst) in enumerate(
            (
                (prolong, stage),
                (mask_h, mask),
                (cols_h, tab.at[pl.ds(0, CAP)]),
                (rows_h, tab.at[pl.ds(T_ROWS, CAP)]),
                (counts_h, counts),
                (fine, blocks.at[pl.ds(0, PANELS)]),
            )
        )
    ]
    for load in loads:
        load.start()

    def remote(src, dst, send, recv, target):
        return pltpu.make_async_remote_copy(
            src_ref=src, dst_ref=dst, send_sem=send, recv_sem=recv, device_id=target, device_id_type=MESH
        )

    for load in loads[:2]:
        load.wait()

    def mask_row(j, carry):
        for e in range(3):
            inside = jnp.logical_and(g + e - 1 >= 0, g + e - 1 < GROUPS)
            keep = jnp.logical_and(mask[e, 0, j] == 1, inside)
            keep = jnp.full((PORES, PORES), jnp.where(keep, 1.0, 0.0), F32).astype(BF16)
            span = pl.ds(e * PORES, PORES)
            held[0, j, :, span] = stage[j, :, span] * keep
        return carry

    lax.fori_loop(0, ROWS, mask_row, 0)
    for load in loads[2:5]:
        load.wait()
    tab[pl.ds(T_COUNT, CAP), :] = jnp.broadcast_to(counts[...], (CAP, PANELS))
    pl.semaphore_wait(barrier, len(friends))

    def tab_copy(n, target):
        return remote(tab, tabs.at[n], tab_send.at[n], tab_recv.at[n], target)

    tab_targets = [minus((0, 0), HELD[n]) for n in range(1, 6)]
    for n in range(1, 6):
        tab_copy(n, device(tab_targets[n - 1])).start()


    def ring_copy(axis, kind):
        next_at, last_at = 1 + 2 * axis, 2 + 2 * axis
        low, high = pl.ds(0, UP[axis]), pl.ds(UP[axis], ROWS - UP[axis])
        up, down = device(HELD[next_at]), device(HELD[last_at])
        src, dst, target = {
            0: (held.at[0, low], held.at[last_at, low], up),
            1: (held.at[0, high], held.at[next_at, high], down),
            2: (held.at[0, high], held.at[last_at, high], up),
            3: (held.at[0, low], held.at[next_at, low], down),
            4: (held.at[last_at, low], far.at[axis, low], up),
            5: (held.at[next_at, high], far.at[axis, high], down),
        }[kind]
        return remote(src, dst, ring_send.at[axis, kind], ring_recv.at[axis, kind], target)

    ring = {(axis, kind): ring_copy(axis, kind) for axis in range(2) for kind in range(6)}
    for kind in range(4):
        for axis in range(2):
            ring[axis, kind].start()

    def turn(n, first=0, last=ROWS):
        def one(j, carry):
            turned[n, j] = (held[n, j] if n < NEAR else far[n - NEAR, j]).T
            return carry

        lax.fori_loop(first, last, one, 0)

    loads[5].wait()

    def list_copy(k):
        panel, worker = SENT[k]
        return remote(blocks.at[at(panel)], blocks.at[PANELS + k], list_send.at[k], list_recv.at[k], device(worker))

    for k in range(FIRST):
        list_copy(k).start()
    turn(0)
    for n in range(1, 6):
        tab_copy(n, device(tab_targets[n - 1])).wait_recv()
    copies = [
        pltpu.make_async_copy(tab, tabs_s.at[0], tab_sem.at[0]),
        pltpu.make_async_copy(tabs.at[pl.ds(1, 5)], tabs_s.at[pl.ds(1, 5)], tab_sem.at[1]),
    ]
    for copy in copies:
        copy.start()
    for copy in copies:
        copy.wait()

    for kind in (0, 1):
        for axis in range(2):
            ring[axis, kind].wait_recv()
            ring[axis, kind + 4].start()
    for k in range(FIRST, len(SENT)):
        list_copy(k).start()
    up_y, up_z = UP
    for n, first, last in ((2, 0, up_y), (4, 0, up_z), (1, up_y, ROWS), (3, up_z, ROWS)):
        turn(n, first, last)
    for kind in (2, 3):
        for axis in range(2):
            ring[axis, kind].wait_recv()
    for n, first, last in ((2, up_y, ROWS), (4, up_z, ROWS), (1, 0, up_y), (3, 0, up_z)):
        turn(n, first, last)

    def gives(slot):
        return (
            remote(give.at[0, slot], got.at[0, slot], give_send.at[0, slot], got_recv.at[0, slot], below),
            remote(give.at[1, slot], got.at[1, slot], give_send.at[1, slot], got_recv.at[1, slot], above),
        )

    def product(source, slot, at_block, lister, column, panel):
        rows = []
        for t in range(CAP):
            live = jnp.where(t < tabs_s[lister, T_COUNT, panel], 1.0, 0.0)
            block = blocks[at_block, t] * jnp.full((PORES, PORES), live, F32).astype(BF16)
            entry = source[column, tabs_s[lister, t, panel]]
            mid[pl.ds(t * PORES, PORES), :] = jnp.dot(block, entry, preferred_element_type=F32).astype(BF16)
            rows.append(turned[lister, tabs_s[lister, T_ROWS + t, panel]])
        total = jnp.dot(jnp.concatenate(rows, axis=1), mid[...], preferred_element_type=F32).astype(BF16)
        give[0, slot] = total[:PORES]
        give[1, slot] = total[2 * PORES :]
        own[slot] = total[PORES : 2 * PORES]
        for copy in gives(slot):
            copy.start()

    def summed(slot):
        for copy in gives(slot):
            copy.wait()

        def block(ref, f):
            return ref[:, pl.ds(f * PORES, PORES)].astype(F32)

        values = []
        for d in range(OFFSETS):
            value = None
            for ref, f in ((own.at[slot], d - 1), (got.at[1, slot], d), (got.at[0, slot], d - 2)):
                if 0 <= f < 3:
                    term = block(ref, f)
                    value = term if value is None else value + term
            values.append(value)
        return values

    def store(values, panel):
        for d, value in enumerate(values):
            out[pl.ds(d * PANELS + panel, PORES, stride=OFFSETS * PANELS), :] = value

    def held_panel(i):
        return at((pick([p[0] for p in HELD], i), pick([p[1] for p in HELD], i)))

    def back(k):
        lister = (pick([HELD[n][0] for n in LISTER], k), pick([HELD[n][1] for n in LISTER], k))
        return remote(result.at[k], returned.at[k], result_send.at[k], result_recv.at[k], device(lister))

    def give_back(k, slot):
        for d, value in enumerate(summed(slot)):
            result[k, :, pl.ds(d * PORES, PORES)] = value.astype(BF16)
        back(k).start()

    def work(i):
        here = (i < LOCAL).astype(jnp.int32)
        k = (i - LOCAL) * (1 - here)
        lister = pick(LISTER, k) * (1 - here)
        column = i * here + pick(COLUMN, k) * (1 - here)
        panel = held_panel(column)
        at_block = panel * here + (PANELS + k) * (1 - here)

        @pl.when(here == 0)
        def _():
            remote(blocks.at[PANELS + k], blocks.at[PANELS + k], list_send.at[k], list_recv.at[k], below).wait_recv()

        @pl.when(column < NEAR)
        def _():
            product(held, i, at_block, lister, column, panel)

        @pl.when(column >= NEAR)
        def _():
            product(far, i, at_block, lister, column - NEAR, panel)

    def finish(i):
        @pl.when(i < LOCAL)
        def _():
            store(summed(i), held_panel(i))

        @pl.when(i >= LOCAL)
        def _():
            give_back(i - LOCAL, i)

    def arrive(k):
        panel = at((pick([p[0] for p, _ in SENT], k), pick([p[1] for p, _ in SENT], k)))
        back(k).wait_recv()
        store([returned[k, :, pl.ds(d * PORES, PORES)].astype(F32) for d in range(OFFSETS)], panel)

    def operate(n, carry):
        kind, i = pick([op for op, _ in ORDER], n), pick([i for _, i in ORDER], n)

        @pl.when(kind == PRODUCT)
        def _():
            work(i)

        @pl.when(kind == SUM)
        def _():
            finish(i)

        @pl.when(kind == RETURN)
        def _():
            arrive(i)

        @pl.when(kind == TURN)
        def _():
            turn(NEAR)

        return carry

    lax.fori_loop(0, FAR_OP, operate, 0)
    for kind in (4, 5):
        for axis in range(2):
            ring[axis, kind].wait_recv()
    lax.fori_loop(FAR_OP, len(ORDER), operate, 0)

    last = len(SENT)

    for n in range(1, 6):
        tab_copy(n, device(tab_targets[n - 1])).wait_send()
    for copy in ring.values():
        copy.wait_send()
    for k in range(last):
        list_copy(k).wait_send()
        back(k).wait_send()


def per_device(fine_blocks, block_rows, block_cols, block_counts, prolong_blocks, prolong_mask):
    any_spec = pl.BlockSpec(memory_space=pl.ANY)
    dma = pltpu.SemaphoreType.DMA
    sent = len(SENT)
    value = pl.pallas_call(
        kernel,
        out_shape=pltpu.VMEM((PORES * OFFSETS * PANELS, PORES), F32),
        in_specs=[any_spec] * 6,
        out_specs=pl.BlockSpec(memory_space=pltpu.VMEM),
        scratch_shapes=[
            pltpu.VMEM((ROWS, PORES, WIDTH), BF16),
            pltpu.VMEM((PANELS + sent, CAP, PORES, PORES), BF16),
            pltpu.VMEM((NEAR, ROWS, PORES, WIDTH), BF16),
            pltpu.VMEM((2, ROWS, PORES, WIDTH), BF16),
            pltpu.VMEM((6, ROWS, WIDTH, PORES), BF16),
            pltpu.VMEM((T_ALL, PANELS), jnp.int32),
            pltpu.VMEM((6, T_ALL, PANELS), jnp.int32),
            pltpu.VMEM((1, PANELS), jnp.int32),
            pltpu.SMEM((3, 1, ROWS), jnp.int32),
            pltpu.SMEM((6, T_ALL, PANELS), jnp.int32),
            pltpu.VMEM((PANELS, PORES, WIDTH), BF16),
            pltpu.VMEM((2, PANELS, PORES, WIDTH), BF16),
            pltpu.VMEM((2, PANELS, PORES, WIDTH), BF16),
            pltpu.VMEM((sent, PORES, OFFSETS * PORES), BF16),
            pltpu.VMEM((sent, PORES, OFFSETS * PORES), BF16),
            pltpu.VMEM((CAP * PORES, WIDTH), BF16),
            dma((6,)),
            dma((6,)),
            dma((6,)),
            dma((2,)),
            dma((2, 6)),
            dma((2, 6)),
            dma((sent,)),
            dma((sent,)),
            dma((2, PANELS)),
            dma((2, PANELS)),
            dma((sent,)),
            dma((sent,)),
        ],
        compiler_params=pltpu.CompilerParams(
            collective_id=0, has_side_effects=True, vmem_limit_bytes=52 * 2**20
        ),
        cost_estimate=pl.CostEstimate(flops=6_500_000_000, bytes_accessed=12_000_000, transcendentals=0),
    )(
        fine_blocks[0, 0],
        prolong_blocks[0],
        block_cols[0, 0].T,
        block_rows[0, 0].T,
        block_counts[0],
        prolong_mask.transpose(2, 0, 1),
    )
    coarse = value.reshape(PORES, OFFSETS, PANELS, PORES).transpose(0, 2, 1, 3)
    return coarse[None, None]


def solution(mesh):
    in_specs = (
        P("rows", "blk", None, None, None, None),
        P("rows", "blk", None, None),
        P("rows", "blk", None, None),
        P("rows", "blk", None),
        P("rows", "blk", None, None),
        P("rows", "blk", None),
    )
    out_specs = P("rows", "blk", None, None, None, None)
    return jax.shard_map(
        per_device, mesh=mesh, in_specs=in_specs, out_specs=out_specs, check_vma=False
    )
```

```python
import jax
import jax.numpy as jnp
from jax import lax
from jax.experimental import pallas as pl
from jax.experimental.pallas import tpu as pltpu
from jax.sharding import PartitionSpec as P

MESH = pl.DeviceIdType.MESH
BF16 = jnp.bfloat16
F32 = jnp.float32
SIDE = 4
ROWS = 16
SPLIT = 10
UP = (10, 9)
CAP = 8
PORES = 128
WIDTH = 384
GROUPS = 8
PANELS = 16
OFFSETS = 5
T_ROWS, T_COUNT, T_ALL = 8, 16, 24
HELD = ((0, 0), (0, 1), (0, 3), (1, 0), (3, 0), (0, 2), (2, 0))
NEAR, LOCAL = 5, 7
SENT = (
    ((2, 2), (0, 2)),
    ((1, 1), (1, 0)),
    ((3, 3), (3, 0)),
    ((1, 3), (0, 3)),
    ((3, 1), (3, 0)),
    ((2, 1), (0, 1)),
    ((2, 3), (0, 3)),
    ((1, 2), (1, 0)),
    ((3, 2), (3, 0)),
)
FIRST = 5


def minus(p, q):
    return (p[0] - q[0]) % SIDE, (p[1] - q[1]) % SIDE


LISTER = tuple(HELD.index(minus((0, 0), h)) for _, h in SENT)
COLUMN = tuple(HELD.index(minus(p, h)) for p, h in SENT)
PRODUCT, SUM, RETURN, TURN = range(4)
ORDER = (
    (PRODUCT, 0),
    (PRODUCT, 1),
    (PRODUCT, 2),
    (PRODUCT, 3),
    (PRODUCT, 4),
    (PRODUCT, 8),
    (PRODUCT, 9),
    (PRODUCT, 10),
    (PRODUCT, 11),
    (SUM, 0),
    (SUM, 1),
    (SUM, 2),
    (SUM, 3),
    (SUM, 4),
    (SUM, 8),
    (SUM, 9),
    (SUM, 10),
    (SUM, 11),
    (TURN, 5),
    (PRODUCT, 7),
    (PRODUCT, 13),
    (PRODUCT, 15),
    (PRODUCT, 12),
    (PRODUCT, 14),
    (SUM, 7),
    (PRODUCT, 5),
    (PRODUCT, 6),
    (SUM, 13),
    (SUM, 15),
    (SUM, 12),
    (SUM, 14),
    (SUM, 5),
    (SUM, 6),
    *((RETURN, k) for k in (0, 1, 2, 3, 4, 6, 8, 5, 7)),
)
FAR_OP = ORDER.index((TURN, 5))


def pick(values, i):
    if isinstance(i, int):
        return values[i]
    words = []
    for first in range(0, len(values), 8):
        word = sum(value << (4 * n) for n, value in enumerate(values[first : first + 8]))
        words.append(word - (1 << 32) if word >= 1 << 31 else word)
    chosen = jnp.int32(words[-1])
    for n in range(len(words) - 2, -1, -1):
        chosen = jnp.where(i < 8 * (n + 1), jnp.int32(words[n]), chosen)
    return lax.shift_right_logical(chosen, (i & 7) * 4) & 15


def kernel(
    fine, prolong, cols_h, rows_h, counts_h, mask_h, out,
    stage, blocks, held, far, turned, tab, tabs, counts, mask, tabs_s,
    own, give, got, result, returned, mid,
    load_sem, tab_send, tab_recv, tab_sem, ring_send, ring_recv, list_send, list_recv, give_send, got_recv,
    result_send, result_recv,
):
    blk, g = lax.axis_index("blk"), lax.axis_index("rows")
    z, y = blk // SIDE, blk % SIDE

    def at(offset):
        dz, dy = offset
        return ((z + dz) % SIDE) * SIDE + (y + dy) % SIDE

    def device(offset):
        return at(offset), g

    below, above = (blk, (g + GROUPS - 1) % GROUPS), (blk, (g + 1) % GROUPS)

    barrier = pltpu.get_barrier_semaphore()
    friends = [device(offset) for offset in HELD[1:6]] + [below, above]
    for friend in friends:
        pl.semaphore_signal(barrier, inc=1, device_id=friend, device_id_type=MESH)

    loads = [
        pltpu.make_async_copy(src, dst, load_sem.at[n])
        for n, (src, dst) in enumerate(
            (
                (mask_h, mask),
                (prolong.at[pl.ds(0, SPLIT)], stage.at[pl.ds(0, SPLIT)]),
                (prolong.at[pl.ds(SPLIT, ROWS - SPLIT)], stage.at[pl.ds(SPLIT, ROWS - SPLIT)]),
                (cols_h, tab.at[pl.ds(0, CAP)]),
                (rows_h, tab.at[pl.ds(T_ROWS, CAP)]),
                (counts_h, counts),
                (fine, blocks.at[pl.ds(0, PANELS)]),
            )
        )
    ]
    for load in loads[:6]:
        load.start()

    def remote(src, dst, send, recv, target):
        return pltpu.make_async_remote_copy(
            src_ref=src, dst_ref=dst, send_sem=send, recv_sem=recv, device_id=target, device_id_type=MESH
        )

    def mask_row(j, carry):
        for e in range(3):
            inside = jnp.logical_and(g + e - 1 >= 0, g + e - 1 < GROUPS)
            keep = jnp.logical_and(mask[e, 0, j] == 1, inside)
            keep = jnp.full((PORES, PORES), jnp.where(keep, 1.0, 0.0), F32).astype(BF16)
            span = pl.ds(e * PORES, PORES)
            held[0, j, :, span] = stage[j, :, span] * keep
        return carry

    for load in loads[:2]:
        load.wait()
    lax.fori_loop(0, SPLIT, mask_row, 0)
    loads[2].wait()
    loads[6].start()
    lax.fori_loop(SPLIT, ROWS, mask_row, 0)
    for load in loads[3:6]:
        load.wait()
    tab[pl.ds(T_COUNT, CAP), :] = jnp.broadcast_to(counts[...], (CAP, PANELS))
    pl.semaphore_wait(barrier, len(friends))

    def tab_copy(n, target):
        return remote(tab, tabs.at[n], tab_send.at[n], tab_recv.at[n], target)

    tab_targets = [minus((0, 0), HELD[n]) for n in range(1, 6)]
    for n in range(1, 6):
        tab_copy(n, device(tab_targets[n - 1])).start()


    def ring_copy(axis, kind):
        next_at, last_at = 1 + 2 * axis, 2 + 2 * axis
        low, high = pl.ds(0, UP[axis]), pl.ds(UP[axis], ROWS - UP[axis])
        up, down = device(HELD[next_at]), device(HELD[last_at])
        src, dst, target = {
            0: (held.at[0, low], held.at[last_at, low], up),
            1: (held.at[0, high], held.at[next_at, high], down),
            2: (held.at[0, high], held.at[last_at, high], up),
            3: (held.at[0, low], held.at[next_at, low], down),
            4: (held.at[last_at, low], far.at[axis, low], up),
            5: (held.at[next_at, high], far.at[axis, high], down),
        }[kind]
        return remote(src, dst, ring_send.at[axis, kind], ring_recv.at[axis, kind], target)

    ring = {(axis, kind): ring_copy(axis, kind) for axis in range(2) for kind in range(6)}
    for kind in range(4):
        for axis in range(2):
            ring[axis, kind].start()

    def turn(n, first=0, last=ROWS):
        def one(j, carry):
            turned[n, j] = (held[n, j] if n < NEAR else far[n - NEAR, j]).T
            return carry

        lax.fori_loop(first, last, one, 0)

    loads[6].wait()

    def list_copy(k):
        panel, worker = SENT[k]
        return remote(blocks.at[at(panel)], blocks.at[PANELS + k], list_send.at[k], list_recv.at[k], device(worker))

    for k in range(FIRST):
        list_copy(k).start()
    turn(0)
    for n in range(1, 6):
        tab_copy(n, device(tab_targets[n - 1])).wait_recv()
    copies = [
        pltpu.make_async_copy(tab, tabs_s.at[0], tab_sem.at[0]),
        pltpu.make_async_copy(tabs.at[pl.ds(1, 5)], tabs_s.at[pl.ds(1, 5)], tab_sem.at[1]),
    ]
    for copy in copies:
        copy.start()
    for copy in copies:
        copy.wait()

    for kind in (0, 1):
        for axis in range(2):
            ring[axis, kind].wait_recv()
            ring[axis, kind + 4].start()
    for k in range(FIRST, len(SENT)):
        list_copy(k).start()
    up_y, up_z = UP
    for n, first, last in ((2, 0, up_y), (4, 0, up_z), (1, up_y, ROWS), (3, up_z, ROWS)):
        turn(n, first, last)
    for kind in (2, 3):
        for axis in range(2):
            ring[axis, kind].wait_recv()
    for n, first, last in ((2, up_y, ROWS), (4, up_z, ROWS), (1, 0, up_y), (3, 0, up_z)):
        turn(n, first, last)

    def gives(slot):
        return (
            remote(give.at[0, slot], got.at[0, slot], give_send.at[0, slot], got_recv.at[0, slot], below),
            remote(give.at[1, slot], got.at[1, slot], give_send.at[1, slot], got_recv.at[1, slot], above),
        )

    def product(source, slot, at_block, lister, column, panel):
        rows = []
        for t in range(CAP):
            live = jnp.where(t < tabs_s[lister, T_COUNT, panel], 1.0, 0.0)
            block = blocks[at_block, t] * jnp.full((PORES, PORES), live, F32).astype(BF16)
            entry = source[column, tabs_s[lister, t, panel]]
            mid[pl.ds(t * PORES, PORES), :] = jnp.dot(block, entry, preferred_element_type=F32).astype(BF16)
            rows.append(turned[lister, tabs_s[lister, T_ROWS + t, panel]])
        total = jnp.dot(jnp.concatenate(rows, axis=1), mid[...], preferred_element_type=F32).astype(BF16)
        give[0, slot] = total[:PORES]
        give[1, slot] = total[2 * PORES :]
        own[slot] = total[PORES : 2 * PORES]
        for copy in gives(slot):
            copy.start()

    def summed(slot):
        for copy in gives(slot):
            copy.wait()

        def block(ref, f):
            return ref[:, pl.ds(f * PORES, PORES)].astype(F32)

        values = []
        for d in range(OFFSETS):
            value = None
            for ref, f in ((own.at[slot], d - 1), (got.at[1, slot], d), (got.at[0, slot], d - 2)):
                if 0 <= f < 3:
                    term = block(ref, f)
                    value = term if value is None else value + term
            values.append(value)
        return values

    def store(values, panel):
        for d, value in enumerate(values):
            out[pl.ds(d * PANELS + panel, PORES, stride=OFFSETS * PANELS), :] = value

    def held_panel(i):
        return at((pick([p[0] for p in HELD], i), pick([p[1] for p in HELD], i)))

    def back(k):
        lister = (pick([HELD[n][0] for n in LISTER], k), pick([HELD[n][1] for n in LISTER], k))
        return remote(result.at[k], returned.at[k], result_send.at[k], result_recv.at[k], device(lister))

    def give_back(k, slot):
        for d, value in enumerate(summed(slot)):
            result[k, :, pl.ds(d * PORES, PORES)] = value.astype(BF16)
        back(k).start()

    def work(i):
        here = (i < LOCAL).astype(jnp.int32)
        k = (i - LOCAL) * (1 - here)
        lister = pick(LISTER, k) * (1 - here)
        column = i * here + pick(COLUMN, k) * (1 - here)
        panel = held_panel(column)
        at_block = panel * here + (PANELS + k) * (1 - here)

        @pl.when(here == 0)
        def _():
            remote(blocks.at[PANELS + k], blocks.at[PANELS + k], list_send.at[k], list_recv.at[k], below).wait_recv()

        @pl.when(column < NEAR)
        def _():
            product(held, i, at_block, lister, column, panel)

        @pl.when(column >= NEAR)
        def _():
            product(far, i, at_block, lister, column - NEAR, panel)

    def finish(i):
        @pl.when(i < LOCAL)
        def _():
            store(summed(i), held_panel(i))

        @pl.when(i >= LOCAL)
        def _():
            give_back(i - LOCAL, i)

    def arrive(k):
        panel = at((pick([p[0] for p, _ in SENT], k), pick([p[1] for p, _ in SENT], k)))
        back(k).wait_recv()
        store([returned[k, :, pl.ds(d * PORES, PORES)].astype(F32) for d in range(OFFSETS)], panel)

    def operate(n, carry):
        kind, i = pick([op for op, _ in ORDER], n), pick([i for _, i in ORDER], n)

        @pl.when(kind == PRODUCT)
        def _():
            work(i)

        @pl.when(kind == SUM)
        def _():
            finish(i)

        @pl.when(kind == RETURN)
        def _():
            arrive(i)

        @pl.when(kind == TURN)
        def _():
            turn(NEAR)

        return carry

    lax.fori_loop(0, FAR_OP, operate, 0)
    for kind in (4, 5):
        for axis in range(2):
            ring[axis, kind].wait_recv()
    lax.fori_loop(FAR_OP, len(ORDER), operate, 0)

    last = len(SENT)

    for n in range(1, 6):
        tab_copy(n, device(tab_targets[n - 1])).wait_send()
    for copy in ring.values():
        copy.wait_send()
    for k in range(last):
        list_copy(k).wait_send()
        back(k).wait_send()


def per_device(fine_blocks, block_rows, block_cols, block_counts, prolong_blocks, prolong_mask):
    any_spec = pl.BlockSpec(memory_space=pl.ANY)
    dma = pltpu.SemaphoreType.DMA
    sent = len(SENT)
    value = pl.pallas_call(
        kernel,
        out_shape=pltpu.VMEM((PORES * OFFSETS * PANELS, PORES), F32),
        in_specs=[any_spec] * 6,
        out_specs=pl.BlockSpec(memory_space=pltpu.VMEM),
        scratch_shapes=[
            pltpu.VMEM((ROWS, PORES, WIDTH), BF16),
            pltpu.VMEM((PANELS + sent, CAP, PORES, PORES), BF16),
            pltpu.VMEM((NEAR, ROWS, PORES, WIDTH), BF16),
            pltpu.VMEM((2, ROWS, PORES, WIDTH), BF16),
            pltpu.VMEM((6, ROWS, WIDTH, PORES), BF16),
            pltpu.VMEM((T_ALL, PANELS), jnp.int32),
            pltpu.VMEM((6, T_ALL, PANELS), jnp.int32),
            pltpu.VMEM((1, PANELS), jnp.int32),
            pltpu.SMEM((3, 1, ROWS), jnp.int32),
            pltpu.SMEM((6, T_ALL, PANELS), jnp.int32),
            pltpu.VMEM((PANELS, PORES, WIDTH), BF16),
            pltpu.VMEM((2, PANELS, PORES, WIDTH), BF16),
            pltpu.VMEM((2, PANELS, PORES, WIDTH), BF16),
            pltpu.VMEM((sent, PORES, OFFSETS * PORES), BF16),
            pltpu.VMEM((sent, PORES, OFFSETS * PORES), BF16),
            pltpu.VMEM((CAP * PORES, WIDTH), BF16),
            dma((7,)),
            dma((6,)),
            dma((6,)),
            dma((2,)),
            dma((2, 6)),
            dma((2, 6)),
            dma((sent,)),
            dma((sent,)),
            dma((2, PANELS)),
            dma((2, PANELS)),
            dma((sent,)),
            dma((sent,)),
        ],
        compiler_params=pltpu.CompilerParams(
            collective_id=0, has_side_effects=True, vmem_limit_bytes=52 * 2**20
        ),
        cost_estimate=pl.CostEstimate(flops=6_500_000_000, bytes_accessed=12_000_000, transcendentals=0),
    )(
        fine_blocks[0, 0],
        prolong_blocks[0],
        block_cols[0, 0].T,
        block_rows[0, 0].T,
        block_counts[0],
        prolong_mask.transpose(2, 0, 1),
    )
    coarse = value.reshape(PORES, OFFSETS, PANELS, PORES).transpose(0, 2, 1, 3)
    return coarse[None, None]


def solution(mesh):
    in_specs = (
        P("rows", "blk", None, None, None, None),
        P("rows", "blk", None, None),
        P("rows", "blk", None, None),
        P("rows", "blk", None),
        P("rows", "blk", None, None),
        P("rows", "blk", None),
    )
    out_specs = P("rows", "blk", None, None, None, None)
    return jax.shard_map(
        per_device, mesh=mesh, in_specs=in_specs, out_specs=out_specs, check_vma=False
    )
```

```python
import jax
import jax.numpy as jnp
from jax import lax
from jax.experimental import pallas as pl
from jax.experimental.pallas import tpu as pltpu
from jax.sharding import PartitionSpec as P

MESH = pl.DeviceIdType.MESH
BF16 = jnp.bfloat16
F32 = jnp.float32
SIDE = 4
ROWS = 16
SPLIT = 10
UP = (10, 9)
CAP = 8
PORES = 128
WIDTH = 384
GROUPS = 8
PANELS = 16
OFFSETS = 5
T_ROWS, T_COUNT, T_ALL = 8, 16, 24
HELD = ((0, 0), (0, 1), (0, 3), (1, 0), (3, 0), (0, 2), (2, 0))
NEAR, LOCAL = 5, 7
SENT = (
    ((2, 2), (0, 2)),
    ((1, 1), (1, 0)),
    ((3, 3), (3, 0)),
    ((1, 3), (0, 3)),
    ((3, 1), (3, 0)),
    ((2, 1), (0, 1)),
    ((2, 3), (0, 3)),
    ((1, 2), (1, 0)),
    ((3, 2), (3, 0)),
)
FIRST = 5


def minus(p, q):
    return (p[0] - q[0]) % SIDE, (p[1] - q[1]) % SIDE


LISTER = tuple(HELD.index(minus((0, 0), h)) for _, h in SENT)
COLUMN = tuple(HELD.index(minus(p, h)) for p, h in SENT)
PRODUCT, SUM, RETURN, TURN = range(4)
ORDER = (
    (PRODUCT, 0),
    (PRODUCT, 1),
    (PRODUCT, 2),
    (PRODUCT, 3),
    (PRODUCT, 4),
    (PRODUCT, 8),
    (PRODUCT, 9),
    (PRODUCT, 10),
    (PRODUCT, 11),
    (SUM, 0),
    (SUM, 1),
    (SUM, 2),
    (SUM, 3),
    (SUM, 4),
    (SUM, 8),
    (SUM, 9),
    (SUM, 10),
    (SUM, 11),
    (TURN, 5),
    (PRODUCT, 7),
    (PRODUCT, 13),
    (PRODUCT, 15),
    (PRODUCT, 12),
    (PRODUCT, 14),
    (SUM, 7),
    (PRODUCT, 5), (SUM, 13), (PRODUCT, 6), (SUM, 15), (SUM, 12), (SUM, 14),
    (SUM, 5), (SUM, 6),
    *((RETURN, k) for k in (0, 1, 2, 3, 4, 6, 8, 5, 7)),
)
FAR_OP = ORDER.index((TURN, 5))


def pick(values, i):
    if isinstance(i, int):
        return values[i]
    words = []
    for first in range(0, len(values), 8):
        word = sum(value << (4 * n) for n, value in enumerate(values[first : first + 8]))
        words.append(word - (1 << 32) if word >= 1 << 31 else word)
    chosen = jnp.int32(words[-1])
    for n in range(len(words) - 2, -1, -1):
        chosen = jnp.where(i < 8 * (n + 1), jnp.int32(words[n]), chosen)
    return lax.shift_right_logical(chosen, (i & 7) * 4) & 15


def kernel(
    fine, prolong, cols_h, rows_h, counts_h, mask_h, out,
    stage, blocks, held, far, turned, tab, tabs, counts, mask, tabs_s,
    own, give, got, result, returned, mid,
    load_sem, tab_send, tab_recv, tab_sem, ring_send, ring_recv, list_send, list_recv, give_send, got_recv,
    result_send, result_recv,
):
    blk, g = lax.axis_index("blk"), lax.axis_index("rows")
    z, y = blk // SIDE, blk % SIDE

    def at(offset):
        dz, dy = offset
        return ((z + dz) % SIDE) * SIDE + (y + dy) % SIDE

    def device(offset):
        return at(offset), g

    below, above = (blk, (g + GROUPS - 1) % GROUPS), (blk, (g + 1) % GROUPS)

    barrier = pltpu.get_barrier_semaphore()
    friends = [device(offset) for offset in HELD[1:6]] + [below, above]
    for friend in friends:
        pl.semaphore_signal(barrier, inc=1, device_id=friend, device_id_type=MESH)

    loads = [
        pltpu.make_async_copy(src, dst, load_sem.at[n])
        for n, (src, dst) in enumerate(
            (
                (mask_h, mask),
                (prolong.at[pl.ds(0, SPLIT)], stage.at[pl.ds(0, SPLIT)]),
                (prolong.at[pl.ds(SPLIT, ROWS - SPLIT)], stage.at[pl.ds(SPLIT, ROWS - SPLIT)]),
                (cols_h, tab.at[pl.ds(0, CAP)]),
                (rows_h, tab.at[pl.ds(T_ROWS, CAP)]),
                (counts_h, counts),
                (fine, blocks.at[pl.ds(0, PANELS)]),
            )
        )
    ]
    for load in loads[:6]:
        load.start()

    def remote(src, dst, send, recv, target):
        return pltpu.make_async_remote_copy(
            src_ref=src, dst_ref=dst, send_sem=send, recv_sem=recv, device_id=target, device_id_type=MESH
        )

    def mask_row(j, carry):
        for e in range(3):
            inside = jnp.logical_and(g + e - 1 >= 0, g + e - 1 < GROUPS)
            keep = jnp.logical_and(mask[e, 0, j] == 1, inside)
            keep = jnp.full((PORES, PORES), jnp.where(keep, 1.0, 0.0), F32).astype(BF16)
            span = pl.ds(e * PORES, PORES)
            held[0, j, :, span] = stage[j, :, span] * keep
        return carry

    for load in loads[:2]:
        load.wait()
    lax.fori_loop(0, SPLIT, mask_row, 0)
    loads[2].wait()
    loads[6].start()
    lax.fori_loop(SPLIT, ROWS, mask_row, 0)
    for load in loads[3:6]:
        load.wait()
    tab[pl.ds(T_COUNT, CAP), :] = jnp.broadcast_to(counts[...], (CAP, PANELS))
    pl.semaphore_wait(barrier, len(friends))

    def tab_copy(n, target):
        return remote(tab, tabs.at[n], tab_send.at[n], tab_recv.at[n], target)

    tab_targets = [minus((0, 0), HELD[n]) for n in range(1, 6)]
    for n in range(1, 6):
        tab_copy(n, device(tab_targets[n - 1])).start()


    def ring_copy(axis, kind):
        next_at, last_at = 1 + 2 * axis, 2 + 2 * axis
        low, high = pl.ds(0, UP[axis]), pl.ds(UP[axis], ROWS - UP[axis])
        up, down = device(HELD[next_at]), device(HELD[last_at])
        src, dst, target = {
            0: (held.at[0, low], held.at[last_at, low], up),
            1: (held.at[0, high], held.at[next_at, high], down),
            2: (held.at[0, high], held.at[last_at, high], up),
            3: (held.at[0, low], held.at[next_at, low], down),
            4: (held.at[last_at, low], far.at[axis, low], up),
            5: (held.at[next_at, high], far.at[axis, high], down),
        }[kind]
        return remote(src, dst, ring_send.at[axis, kind], ring_recv.at[axis, kind], target)

    ring = {(axis, kind): ring_copy(axis, kind) for axis in range(2) for kind in range(6)}
    for kind in range(4):
        for axis in range(2):
            ring[axis, kind].start()

    def turn(n, first=0, last=ROWS):
        def one(j, carry):
            turned[n, j] = (held[n, j] if n < NEAR else far[n - NEAR, j]).T
            return carry

        lax.fori_loop(first, last, one, 0)

    loads[6].wait()

    def list_copy(k):
        panel, worker = SENT[k]
        return remote(blocks.at[at(panel)], blocks.at[PANELS + k], list_send.at[k], list_recv.at[k], device(worker))

    for k in range(FIRST):
        list_copy(k).start()
    turn(0)
    for n in range(1, 6):
        tab_copy(n, device(tab_targets[n - 1])).wait_recv()
    copies = [
        pltpu.make_async_copy(tab, tabs_s.at[0], tab_sem.at[0]),
        pltpu.make_async_copy(tabs.at[pl.ds(1, 5)], tabs_s.at[pl.ds(1, 5)], tab_sem.at[1]),
    ]
    for copy in copies:
        copy.start()
    for copy in copies:
        copy.wait()

    for kind in (0, 1):
        for axis in range(2):
            ring[axis, kind].wait_recv()
            ring[axis, kind + 4].start()
    for k in range(FIRST, len(SENT)):
        list_copy(k).start()
    up_y, up_z = UP
    for n, first, last in ((2, 0, up_y), (4, 0, up_z), (1, up_y, ROWS), (3, up_z, ROWS)):
        turn(n, first, last)
    for kind in (2, 3):
        for axis in range(2):
            ring[axis, kind].wait_recv()
    for n, first, last in ((2, up_y, ROWS), (4, up_z, ROWS), (1, 0, up_y), (3, 0, up_z)):
        turn(n, first, last)

    def gives(slot):
        return (
            remote(give.at[0, slot], got.at[0, slot], give_send.at[0, slot], got_recv.at[0, slot], below),
            remote(give.at[1, slot], got.at[1, slot], give_send.at[1, slot], got_recv.at[1, slot], above),
        )

    def product(source, slot, at_block, lister, column, panel):
        rows = []
        for t in range(CAP):
            live = jnp.where(t < tabs_s[lister, T_COUNT, panel], 1.0, 0.0)
            block = blocks[at_block, t] * jnp.full((PORES, PORES), live, F32).astype(BF16)
            entry = source[column, tabs_s[lister, t, panel]]
            mid[pl.ds(t * PORES, PORES), :] = jnp.dot(block, entry, preferred_element_type=F32).astype(BF16)
            rows.append(turned[lister, tabs_s[lister, T_ROWS + t, panel]])
        total = jnp.dot(jnp.concatenate(rows, axis=1), mid[...], preferred_element_type=F32).astype(BF16)
        give[0, slot] = total[:PORES]
        give[1, slot] = total[2 * PORES :]
        own[slot] = total[PORES : 2 * PORES]
        for copy in gives(slot):
            copy.start()

    def summed(slot):
        for copy in gives(slot):
            copy.wait()

        def block(ref, f):
            return ref[:, pl.ds(f * PORES, PORES)].astype(F32)

        values = []
        for d in range(OFFSETS):
            value = None
            for ref, f in ((own.at[slot], d - 1), (got.at[1, slot], d), (got.at[0, slot], d - 2)):
                if 0 <= f < 3:
                    term = block(ref, f)
                    value = term if value is None else value + term
            values.append(value)
        return values

    def store(values, panel):
        for d, value in enumerate(values):
            out[pl.ds(d * PANELS + panel, PORES, stride=OFFSETS * PANELS), :] = value

    def held_panel(i):
        return at((pick([p[0] for p in HELD], i), pick([p[1] for p in HELD], i)))

    def back(k):
        lister = (pick([HELD[n][0] for n in LISTER], k), pick([HELD[n][1] for n in LISTER], k))
        return remote(result.at[k], returned.at[k], result_send.at[k], result_recv.at[k], device(lister))

    def give_back(k, slot):
        for d, value in enumerate(summed(slot)):
            result[k, :, pl.ds(d * PORES, PORES)] = value.astype(BF16)
        back(k).start()

    def work(i):
        here = (i < LOCAL).astype(jnp.int32)
        k = (i - LOCAL) * (1 - here)
        lister = pick(LISTER, k) * (1 - here)
        column = i * here + pick(COLUMN, k) * (1 - here)
        panel = held_panel(column)
        at_block = panel * here + (PANELS + k) * (1 - here)

        @pl.when(here == 0)
        def _():
            remote(blocks.at[PANELS + k], blocks.at[PANELS + k], list_send.at[k], list_recv.at[k], below).wait_recv()

        @pl.when(column < NEAR)
        def _():
            product(held, i, at_block, lister, column, panel)

        @pl.when(column >= NEAR)
        def _():
            product(far, i, at_block, lister, column - NEAR, panel)

    def finish(i):
        @pl.when(i < LOCAL)
        def _():
            store(summed(i), held_panel(i))

        @pl.when(i >= LOCAL)
        def _():
            give_back(i - LOCAL, i)

    def arrive(k):
        panel = at((pick([p[0] for p, _ in SENT], k), pick([p[1] for p, _ in SENT], k)))
        back(k).wait_recv()
        store([returned[k, :, pl.ds(d * PORES, PORES)].astype(F32) for d in range(OFFSETS)], panel)

    def operate(n, carry):
        kind, i = pick([op for op, _ in ORDER], n), pick([i for _, i in ORDER], n)

        @pl.when(kind == PRODUCT)
        def _():
            work(i)

        @pl.when(kind == SUM)
        def _():
            finish(i)

        @pl.when(kind == RETURN)
        def _():
            arrive(i)

        @pl.when(kind == TURN)
        def _():
            turn(NEAR)

        return carry

    lax.fori_loop(0, FAR_OP, operate, 0)
    for kind in (4, 5):
        for axis in range(2):
            ring[axis, kind].wait_recv()
    lax.fori_loop(FAR_OP, len(ORDER), operate, 0)

    last = len(SENT)

    for n in range(1, 6):
        tab_copy(n, device(tab_targets[n - 1])).wait_send()
    for copy in ring.values():
        copy.wait_send()
    for k in range(last):
        list_copy(k).wait_send()
        back(k).wait_send()


def per_device(fine_blocks, block_rows, block_cols, block_counts, prolong_blocks, prolong_mask):
    any_spec = pl.BlockSpec(memory_space=pl.ANY)
    dma = pltpu.SemaphoreType.DMA
    sent = len(SENT)
    value = pl.pallas_call(
        kernel,
        out_shape=pltpu.VMEM((PORES * OFFSETS * PANELS, PORES), F32),
        in_specs=[any_spec] * 6,
        out_specs=pl.BlockSpec(memory_space=pltpu.VMEM),
        scratch_shapes=[
            pltpu.VMEM((ROWS, PORES, WIDTH), BF16),
            pltpu.VMEM((PANELS + sent, CAP, PORES, PORES), BF16),
            pltpu.VMEM((NEAR, ROWS, PORES, WIDTH), BF16),
            pltpu.VMEM((2, ROWS, PORES, WIDTH), BF16),
            pltpu.VMEM((6, ROWS, WIDTH, PORES), BF16),
            pltpu.VMEM((T_ALL, PANELS), jnp.int32),
            pltpu.VMEM((6, T_ALL, PANELS), jnp.int32),
            pltpu.VMEM((1, PANELS), jnp.int32),
            pltpu.SMEM((3, 1, ROWS), jnp.int32),
            pltpu.SMEM((6, T_ALL, PANELS), jnp.int32),
            pltpu.VMEM((PANELS, PORES, WIDTH), BF16),
            pltpu.VMEM((2, PANELS, PORES, WIDTH), BF16),
            pltpu.VMEM((2, PANELS, PORES, WIDTH), BF16),
            pltpu.VMEM((sent, PORES, OFFSETS * PORES), BF16),
            pltpu.VMEM((sent, PORES, OFFSETS * PORES), BF16),
            pltpu.VMEM((CAP * PORES, WIDTH), BF16),
            dma((7,)),
            dma((6,)),
            dma((6,)),
            dma((2,)),
            dma((2, 6)),
            dma((2, 6)),
            dma((sent,)),
            dma((sent,)),
            dma((2, PANELS)),
            dma((2, PANELS)),
            dma((sent,)),
            dma((sent,)),
        ],
        compiler_params=pltpu.CompilerParams(
            collective_id=0, has_side_effects=True, vmem_limit_bytes=52 * 2**20
        ),
        cost_estimate=pl.CostEstimate(flops=6_500_000_000, bytes_accessed=12_000_000, transcendentals=0),
    )(
        fine_blocks[0, 0],
        prolong_blocks[0],
        block_cols[0, 0].T,
        block_rows[0, 0].T,
        block_counts[0],
        prolong_mask.transpose(2, 0, 1),
    )
    coarse = value.reshape(PORES, OFFSETS, PANELS, PORES).transpose(0, 2, 1, 3)
    return coarse[None, None]


def solution(mesh):
    in_specs = (
        P("rows", "blk", None, None, None, None),
        P("rows", "blk", None, None),
        P("rows", "blk", None, None),
        P("rows", "blk", None),
        P("rows", "blk", None, None),
        P("rows", "blk", None),
    )
    out_specs = P("rows", "blk", None, None, None, None)
    return jax.shard_map(
        per_device, mesh=mesh, in_specs=in_specs, out_specs=out_specs, check_vma=False
    )
```
